32 devices in a mesh: batch: 16 (over z, y, x), fsdp: 2 (over core).
Axes of the slice: x: 2, y: 2, z: 4, core: 2. Of those that a mesh axis runs over, the one named last changes fastest.
Arguments:
- frames: bfloat16 [16, 1024, 1024], P('batch', 'fsdp'), may hold values from -6 to 6
- segment_ids: int32 [16, 1024], P('batch'), may hold values from 0 to 3, never falling along the last dimension, each value on 1 to 512 neighbouring positions
- valid_mask: int32 [16, 1024], P('batch'), may hold values 0 or 1
- first_norm: float32 [1024], replicated, may hold values from 0.5 to 1.5
- first_up: bfloat16 [4096, 1024], P('fsdp'), may hold values from -0.1875 to 0.1875
- first_down: bfloat16 [4096, 1024], P('fsdp'), may hold values from -0.1875 to 0.1875
- attention_norm: float32 [1024], replicated, may hold values from 0.5 to 1.5
- query_proj: bfloat16 [1024, 1024], P('fsdp'), may hold values from -0.1875 to 0.1875
- key_proj: bfloat16 [1024, 1024], P('fsdp'), may hold values from -0.1875 to 0.1875
- value_proj: bfloat16 [1024, 1024], P('fsdp'), may hold values from -0.1875 to 0.1875
- output_proj: bfloat16 [1024, 1024], P('fsdp'), may hold values from -3 to 3
- position_proj: bfloat16 [1024, 1024], P('fsdp'), may hold values from -0.1875 to 0.1875
- content_bias: float32 [1024], replicated, may hold values from -3 to 3
- position_bias: float32 [1024], replicated, may hold values from -3 to 3
- convolution_norm: float32 [1024], replicated, may hold values from 0.5 to 1.5
- pointwise_in: bfloat16 [1024, 2048], P('fsdp'), may hold values from -0.1875 to 0.1875
- depthwise: float32 [1024, 5], replicated, may hold values from -2.5 to 2.5
- batch_gain: float32 [1024], replicated, may hold values from 0.5 to 1.5
- batch_shift: float32 [1024], replicated, may hold values from -3 to 3
- pointwise_out: bfloat16 [1024, 1024], P('fsdp'), may hold values from -0.1875 to 0.1875
- second_norm: float32 [1024], replicated, may hold values from 0.5 to 1.5
- second_up: bfloat16 [4096, 1024], P('fsdp'), may hold values from -0.1875 to 0.1875
- second_down: bfloat16 [4096, 1024], P('fsdp'), may hold values from -0.1875 to 0.1875
- final_norm: float32 [1024], replicated, may hold values from 0.5 to 1.5
- cotangent: bfloat16 [16, 1024, 1024], P('batch', 'fsdp'), may hold values from -6 to 6
Outputs:
- layer_out: bfloat16 [16, 1024, 1024], P('batch', 'fsdp')
- frames_grad: bfloat16 [16, 1024, 1024], P('batch', 'fsdp')
- first_norm_grad: float32 [1024], P('fsdp')
- first_up_grad: float32 [4096, 1024], P('fsdp')
- first_down_grad: float32 [4096, 1024], P('fsdp')
- attention_norm_grad: float32 [1024], P('fsdp')
- query_proj_grad: float32 [1024, 1024], P('fsdp')
- key_proj_grad: float32 [1024, 1024], P('fsdp')
- value_proj_grad: float32 [1024, 1024], P('fsdp')
- output_proj_grad: float32 [1024, 1024], P('fsdp')
- position_proj_grad: float32 [1024, 1024], P('fsdp')
- content_bias_grad: float32 [1024], P('fsdp')
- position_bias_grad: float32 [1024], P('fsdp')
- convolution_norm_grad: float32 [1024], P('fsdp')
- pointwise_in_grad: float32 [1024, 2048], P('fsdp')
- depthwise_grad: float32 [1024, 5], P('fsdp')
- batch_gain_grad: float32 [1024], P('fsdp')
- batch_shift_grad: float32 [1024], P('fsdp')
- pointwise_out_grad: float32 [1024, 1024], P('fsdp')
- second_norm_grad: float32 [1024], P('fsdp')
- second_up_grad: float32 [4096, 1024], P('fsdp')
- second_down_grad: float32 [4096, 1024], P('fsdp')
- final_norm_grad: float32 [1024], P('fsdp')
The draws below stay inside these ranges and needn't reach their ends.
Inputs may be any that keep to these rules, and one draw needn't show every extreme that they name: `segment_ids`: segment numbers never fall along a row; each utterance of a row has 1 to 512 frames.
All inputs are finite; a program needn't handle non-finite values. No bound on the sum of `valid_mask` on one device may be relied on, other than what follows from the above.
Results may differ from the reference program's by a relative error of at most 0.035.
Values may be sent and summed in bfloat16 or wider, within the bound.
No kernel may reach another device: no remote copies, remote signals or barrier semaphores. Data moves between devices by JAX's collectives and lax.ppermute only.
A program may use at most 384 MiB of HBM per device.

```python
import math
import jax
import jax.numpy as jnp
import numpy as np
from jax import lax

D = 1024
H = 8
DH = 128
FF = 4096
KER = 5
LEN = 1024
UTT = 4
ROWS = 16


def set_ends(drawn, rng, low, largest):
    shape = drawn.shape
    place = [jax.random.randint(jax.random.fold_in(rng, axis), (), 0, shape[axis]) for axis in range(len(shape))]
    drawn = drawn.at[tuple(place)].set(low)
    longest = shape.index(max(shape))
    place[longest] = (place[longest] + 1) % shape[longest]
    return drawn.at[tuple(place)].set(largest)


def level_of(own_key, extent, split, smallest, largest):
    gain = 1.0
    for position, parts in split:
        steps = jax.random.uniform(jax.random.fold_in(jax.random.fold_in(own_key, 6), position), (parts,), jnp.float32, smallest / len(split), largest / len(split))
        gain = gain * jnp.repeat(jnp.exp(steps), extent[position] // parts).reshape((-1,) + (1,) * (len(extent) - 1 - position))
    return gain


def length_profile(amount, total, limit, skew):
    weights = [(1 << 20) // math.isqrt(rank ** skew) + 1 for rank in range(2, amount + 1)]
    surplus, counts = total - limit - (amount - 1), [1] * (amount - 1)
    while surplus > 0:
        movable = [i for i in range(amount - 1) if counts[i] < limit]
        pool, budget = sum([weights[i] for i in movable]), surplus
        for i in movable:
            more = min(limit - counts[i], max(1, budget * weights[i] // pool), surplus)
            counts[i] = counts[i] + more
            surplus = surplus - more
    return np.array([limit] + counts)


def uneven(own_key, number_of, total, reach, skew):
    if number_of == 2:
        one = jax.random.randint(own_key, (), max(1, total - reach), min(reach, total - 1) + 1)
        return jnp.stack([one, total - one])
    lengths = jnp.asarray(length_profile(number_of, total, reach, skew), jnp.int32)
    twos = (number_of - 1) // 2
    giver, sink = lengths[1:1 + 2 * twos:2], lengths[2:2 + 2 * twos:2]
    room = jnp.minimum(giver - 1, reach - sink)
    shifted = jax.random.randint(jax.random.fold_in(own_key, 1), (twos,), 0, 1 << 20) % (room + 1)
    lengths = lengths.at[1:1 + 2 * twos:2].set(giver - shifted).at[2:2 + 2 * twos:2].set(sink + shifted)
    return lengths[jax.random.permutation(jax.random.fold_in(own_key, 2), number_of)]


def gaussian(own_key, shape, spread, most, split=(), held_as=jnp.bfloat16):
    entries = spread * jax.random.normal(own_key, shape, jnp.float32)
    if split:
        entries = entries * level_of(own_key, shape, split, -0.22, 0.18)
    return jnp.clip(entries, -most, most).astype(held_as)


def setup_inputs(seed: int = 0) -> dict:
    seeds = jax.random.split(jax.random.key(seed), 26)
    return {
        "frames": gaussian(seeds[0], (ROWS, LEN, D), 1.0, 6.0, ((0, 16), (1, 2))),
        "segment_ids": jax.vmap(lambda own: jnp.searchsorted(jnp.cumsum(uneven(own, UTT, LEN, LEN // 2, 1)), jnp.arange(LEN), side="right"))(jax.random.split(seeds[1], ROWS)).reshape((ROWS, LEN)).astype(jnp.int32),
        "valid_mask": set_ends((jax.random.randint(seeds[2], (ROWS, LEN), 0, 2) < 1).astype(jnp.int32), jax.random.fold_in(seeds[2], 1), 0, 1),
        "first_norm": jnp.clip(1.0 + 0.1 * jax.random.normal(seeds[3], (D,), jnp.float32), 0.5, 1.5),
        "first_up": gaussian(seeds[4], (FF, D), D ** -0.5, 0.1875, ((0, 2),)),
        "first_down": gaussian(seeds[5], (FF, D), (FF // 4) ** -0.5, 0.1875, ((0, 2),)),
        "attention_norm": jnp.clip(1.0 + 0.1 * jax.random.normal(seeds[6], (D,), jnp.float32), 0.5, 1.5),
        "query_proj": gaussian(seeds[7], (D, D), D ** -0.5, 0.1875, ((0, 2),)),
        "key_proj": gaussian(seeds[8], (D, D), D ** -0.5, 0.1875, ((0, 2),)),
        "value_proj": gaussian(seeds[9], (D, D), D ** -0.5, 0.1875, ((0, 2),)),
        "output_proj": gaussian(seeds[10], (D, D), (D * 4 // LEN) ** -0.5, 3.0, ((0, 2),)),
        "position_proj": gaussian(seeds[11], (D, D), D ** -0.5, 0.1875, ((0, 2),)),
        "content_bias": gaussian(seeds[12], (D,), 0.5, 3.0, (), jnp.float32),
        "position_bias": gaussian(seeds[13], (D,), 0.5, 3.0, (), jnp.float32),
        "convolution_norm": jnp.clip(1.0 + 0.1 * jax.random.normal(seeds[14], (D,), jnp.float32), 0.5, 1.5),
        "pointwise_in": gaussian(seeds[15], (D, 2 * D), D ** -0.5, 0.1875, ((0, 2),)),
        "depthwise": gaussian(seeds[16], (D, KER), KER ** -0.5, 2.5, (), jnp.float32),
        "batch_gain": jnp.clip(1.0 + 0.1 * jax.random.normal(seeds[17], (D,), jnp.float32), 0.5, 1.5),
        "batch_shift": gaussian(seeds[18], (D,), 0.5, 3.0, (), jnp.float32),
        "pointwise_out": gaussian(seeds[19], (D, D), D ** -0.5, 0.1875, ((0, 2),)),
        "second_norm": jnp.clip(1.0 + 0.1 * jax.random.normal(seeds[20], (D,), jnp.float32), 0.5, 1.5),
        "second_up": gaussian(seeds[21], (FF, D), D ** -0.5, 0.1875, ((0, 2),)),
        "second_down": gaussian(seeds[22], (FF, D), (FF // 4) ** -0.5, 0.1875, ((0, 2),)),
        "final_norm": jnp.clip(1.0 + 0.1 * jax.random.normal(seeds[23], (D,), jnp.float32), 0.5, 1.5),
        "cotangent": gaussian(seeds[24], (ROWS, LEN, D), 1.0, 6.0, ((0, 16), (1, 2))),
    }


@jax.custom_vjp
def low(v):
    return lax.optimization_barrier(v.astype(jnp.bfloat16)).astype(jnp.float32)

@jax.custom_vjp
def low_back(v):
    return v

def low_keep(v):
    return (low(v), None)

def low_pass(kept, grad):
    return (grad,)

def back_keep(v):
    return (v, None)

def back_low(kept, grad):
    return (low(grad),)
low.defvjp(low_keep, low_pass)
low_back.defvjp(back_keep, back_low)
epsilon = 1e-05
neg_big = -1e+30
exact = lax.Precision.HIGHEST

def layer_norm(values, norm_gain):
    average = lax.optimization_barrier(jnp.mean(values, axis=-1, keepdims=True))
    centred = values - average
    inverse_dev = lax.rsqrt(lax.optimization_barrier(jnp.mean(centred * centred, axis=-1, keepdims=True)) + epsilon)
    return centred * inverse_dev * norm_gain

def encoding(distance, features):
    half_width = features // 2
    channel = jnp.arange(half_width).astype(jnp.float32)
    frequency = jnp.exp(channel * (-2.0 * math.log(10000.0) / features))
    angles = distance[:, None] * frequency[None, :]
    return jnp.concatenate([jnp.sin(angles), jnp.cos(angles)], axis=1)

def rel_shift(full_window, queries, keys_count):
    leading = full_window.shape[:-2]
    window = full_window.shape[-1]
    flattened = full_window.reshape(leading + (queries * window,))
    flattened = flattened[..., queries - 1:queries - 1 + queries * (window - 1)]
    return flattened.reshape(leading + (queries, window - 1))[..., :keys_count]

def project(activity, matrix):
    return jnp.einsum('bld,de->ble', activity, matrix, precision=exact, preferred_element_type=jnp.float32)

def feed_forward(source, norm_gain, up_matrix, down_matrix):
    lowered = low(layer_norm(source, norm_gain))
    hidden_pre = low_back(jnp.einsum('bld,fd->blf', lowered, up_matrix, precision=exact, preferred_element_type=jnp.float32))
    hidden = low(jax.nn.silu(hidden_pre))
    branch = low_back(jnp.einsum('blf,fd->bld', hidden, down_matrix, precision=exact, preferred_element_type=jnp.float32))
    return source + 0.5 * branch

def attention(source, segments, norm_gain, query_matrix, key_matrix, value_matrix, output_matrix, content_vec, position_vec, pos_heads):
    batch_rows = source.shape[0]
    lowered = low(layer_norm(source, norm_gain))
    queries = low_back(project(lowered, query_matrix))
    key_heads = low(low_back(project(lowered, key_matrix))).reshape(batch_rows, LEN, H, DH)
    value_heads = low(low_back(project(lowered, value_matrix))).reshape(batch_rows, LEN, H, DH)
    query_content = low(queries + content_vec).reshape(batch_rows, LEN, H, DH)
    query_position = low(queries + position_vec).reshape(batch_rows, LEN, H, DH)
    content = jnp.einsum('rihe,rjhe->rhij', query_content, key_heads, precision=exact, preferred_element_type=jnp.float32)
    full_window = jnp.einsum('rihe,uhe->rhiu', query_position, pos_heads, precision=exact, preferred_element_type=jnp.float32)
    summed = low_back(content + rel_shift(full_window, LEN, LEN))
    same_utterance = (segments[:, :, None] == segments[:, None, :])[:, None]
    masked = jnp.where(same_utterance, summed * (1.0 / math.sqrt(DH)), neg_big)
    probabilities = low(jax.nn.softmax(masked, axis=-1))
    context = jnp.einsum('rhij,rjhe->rihe', probabilities, value_heads, precision=exact, preferred_element_type=jnp.float32)
    context = low(low_back(context)).reshape(batch_rows, LEN, D)
    return source + low_back(project(context, output_matrix))

def depthwise_conv(gated_vals, segments, kernel):
    rim_width = (KER - 1) // 2
    rimmed = jnp.pad(gated_vals, ((0, 0), (rim_width, rim_width), (0, 0)))
    seg_rim = jnp.pad(segments, ((0, 0), (rim_width, rim_width)), constant_values=-1)
    depth_out = jnp.zeros_like(gated_vals)
    for offset in range(KER):
        linked = (seg_rim[:, offset:offset + LEN] == segments).astype(jnp.float32)[:, :, None]
        depth_out = depth_out + rimmed[:, offset:offset + LEN] * linked * kernel[:, offset]
    return depth_out

def early_part(params, source, segments):
    first_norm, first_up, first_down, attention_norm, query_proj, key_proj, value_proj, output_proj, content_bias, position_bias, convolution_norm, pointwise_in, depthwise, pos_heads = params
    after_first = feed_forward(source, first_norm, first_up, first_down)
    after_attention = attention(after_first, segments, attention_norm, query_proj, key_proj, value_proj, output_proj, content_bias, position_bias, pos_heads)
    lowered = low(layer_norm(after_attention, convolution_norm))
    gate_in = low_back(project(lowered, pointwise_in))
    gated_vals = gate_in[..., :D] * jax.nn.sigmoid(gate_in[..., D:])
    return (after_attention, depthwise_conv(gated_vals, segments, depthwise))

def late_part(params, source, depth_out):
    average, inverse_dev, batch_gain, batch_shift, pointwise_out, second_norm, second_up, second_down, final_norm = params
    standard = (depth_out - average) * inverse_dev
    swished = low(jax.nn.silu(standard * batch_gain + batch_shift))
    after_conv = source + low_back(project(swished, pointwise_out))
    after_second = feed_forward(after_conv, second_norm, second_up, second_down)
    return layer_norm(after_second, final_norm)

def forward(source, segments, valid, weights):
    first_norm, first_up, first_down, attention_norm, query_proj, key_proj, value_proj, output_proj, position_proj, content_bias, position_bias, convolution_norm, pointwise_in, depthwise, batch_gain, batch_shift, pointwise_out, second_norm, second_up, second_down, final_norm = weights
    group_rows = math.gcd(ROWS, 2)
    blocks = ROWS // group_rows
    distance = (LEN - 1 - jnp.arange(2 * LEN)).astype(jnp.float32)
    positions = low(encoding(distance, D))
    pos_heads = low(jnp.dot(positions, position_proj, precision=exact, preferred_element_type=jnp.float32)).reshape(2 * LEN, H, DH)
    early_params = (first_norm, first_up, first_down, attention_norm, query_proj, key_proj, value_proj, output_proj, content_bias, position_bias, convolution_norm, pointwise_in, depthwise, pos_heads)
    early_fn = jax.checkpoint(early_part)

    def early_step(carry, inputs):
        return (carry, early_fn(early_params, inputs[0], inputs[1]))
    unused, (mixed, depth_all) = lax.scan(early_step, jnp.zeros((), jnp.float32), (source.reshape(blocks, group_rows, LEN, D), segments.reshape(blocks, group_rows, LEN)))
    depth_flat = depth_all.reshape(ROWS, LEN, D)
    valid_col = valid[:, :, None]
    count = jnp.sum(valid)
    average = lax.optimization_barrier(jnp.sum(valid_col * depth_flat, axis=(0, 1))) / count
    second = lax.optimization_barrier(jnp.sum(valid_col * depth_flat * depth_flat, axis=(0, 1))) / count
    inverse_dev = lax.rsqrt(second - average * average + epsilon)
    late_params = (average, inverse_dev, batch_gain, batch_shift, pointwise_out, second_norm, second_up, second_down, final_norm)
    late_fn = jax.checkpoint(late_part)

    def late_step(carry, inputs):
        return (carry, late_fn(late_params, inputs[0], inputs[1]))
    unused, outputs = lax.scan(late_step, jnp.zeros((), jnp.float32), (mixed, depth_all))
    return outputs.reshape(ROWS, LEN, D)

def reference(frames, segment_ids, valid_mask, first_norm, first_up, first_down, attention_norm, query_proj, key_proj, value_proj, output_proj, position_proj, content_bias, position_bias, convolution_norm, pointwise_in, depthwise, batch_gain, batch_shift, pointwise_out, second_norm, second_up, second_down, final_norm, cotangent):
    weights = tuple((item.astype(jnp.float32) for item in (first_norm, first_up, first_down, attention_norm, query_proj, key_proj, value_proj, output_proj, position_proj, content_bias, position_bias, convolution_norm, pointwise_in, depthwise, batch_gain, batch_shift, pointwise_out, second_norm, second_up, second_down, final_norm)))
    valid = valid_mask.astype(jnp.float32)

    def whole(source, *params):
        return forward(source, segment_ids, valid, params)
    result, pullback = jax.vjp(whole, frames.astype(jnp.float32), *weights)
    grads = pullback(cotangent.astype(jnp.float32))
    return (result.astype(jnp.bfloat16), grads[0].astype(jnp.bfloat16), grads[1], grads[2], grads[3], grads[4], grads[5], grads[6], grads[7], grads[8], grads[9], grads[10], grads[11], grads[12], grads[13], grads[14], grads[15], grads[16], grads[17], grads[18], grads[19], grads[20], grads[21])
```

```python
import functools
import math

import jax
import jax.numpy as jnp
from jax import lax
from jax.experimental import pallas as pl
from jax.experimental.pallas import tpu as pltpu
from jax.sharding import PartitionSpec as P

H = 8
DH = 128
KER = 5
RIM = (KER - 1) // 2
EPS = 1e-05
NEG = -1e30
BF = jnp.bfloat16
F32 = jnp.float32
VMEM = 56 * 1024 * 1024


def dot(a, b, da=1, db=0):
    return lax.dot_general(a, b, (((da,), (db,)), ((), ())), preferred_element_type=F32)


def norm_parts(v):
    centred = v - jnp.mean(v, axis=-1, keepdims=True)
    rstd = lax.rsqrt(jnp.mean(centred * centred, axis=-1, keepdims=True) + EPS)
    return centred * rstd, rstd


def norm_back(grad, hat, rstd, gain):
    scaled = grad * gain
    first = jnp.mean(scaled, axis=-1, keepdims=True)
    second = jnp.mean(scaled * hat, axis=-1, keepdims=True)
    return rstd * (scaled - first - hat * second)


def slope(v):
    s = jax.nn.sigmoid(v)
    return s * (1.0 + v * (1.0 - s))


def shifted(v, s):
    g = lax.axis_size("fsdp")
    return lax.ppermute(v, "fsdp", [(i, (i + s) % g) for i in range(g)])


def natural(blocks):
    g = len(blocks)
    me = lax.axis_index("fsdp")
    if g == 1:
        return blocks[0][None]
    if g == 2:
        a, b = blocks
        return jnp.where(me == 0, jnp.stack([a, b]), jnp.stack([b, a]))
    stacked = jnp.stack(blocks[::-1])
    return jnp.roll(stacked, me + 1, axis=0)


def gather_rows(v):
    g = lax.axis_size("fsdp")
    out = natural([v] + [shifted(v, s) for s in range(1, g)])
    return out.reshape((g * v.shape[0],) + v.shape[1:])


def pair_sum(v):
    g = lax.axis_size("fsdp")
    total = v.astype(F32)
    for s in range(1, g):
        total = total + shifted(v, s).astype(F32)
    return total


def pair_scatter(v):
    g = lax.axis_size("fsdp")
    me = lax.axis_index("fsdp")
    n = v.shape[0] // g
    total = lax.dynamic_slice_in_dim(v, me * n, n, 0).astype(F32)
    for s in range(1, g):
        other = lax.dynamic_slice_in_dim(v, lax.rem(me + s, g) * n, n, 0)
        total = total + shifted(other, s).astype(F32)
    return total


def row_blocks_swap(v):
    g = lax.axis_size("fsdp")
    me = lax.axis_index("fsdp")
    n = v.shape[0] // g
    blocks = [lax.dynamic_slice_in_dim(v, me * n, n, 0)]
    for s in range(1, g):
        blocks.append(shifted(lax.dynamic_slice_in_dim(v, lax.rem(me + s, g) * n, n, 0), s))
    return natural(blocks)


def own_columns(matrices):
    g = lax.axis_size("fsdp")
    me = lax.axis_index("fsdp")

    def columns(member):
        parts = []
        for m, width in matrices:
            parts.append(lax.dynamic_slice_in_dim(m, member * width, width, 1))
        return jnp.concatenate(parts, axis=1)

    blocks = [columns(me)]
    for s in range(1, g):
        blocks.append(shifted(columns(lax.rem(me + s, g)), s))
    out = natural(blocks)
    return out.reshape((-1, out.shape[-1]))


def bit_of(b):
    return (lax.axis_index("batch") >> b) & 1


def exchange(v, b):
    n = lax.axis_size("batch")
    return lax.ppermute(v, "batch", [(i, i ^ (1 << b)) for i in range(n)])


def is_power(n):
    return n & (n - 1) == 0


def row_sum(v):
    n = lax.axis_size("batch")
    if not is_power(n):
        return lax.psum(v, "batch")
    for b in range(n.bit_length() - 1):
        v = v + exchange(v, b)
    return v


def orders():
    bits = lax.axis_size("batch").bit_length() - 1
    if bits == 4:
        return ([0, 2, 1, 3], [1, 2, 0, 3])
    rest = list(range(bits))
    return (rest, rest[1:] + rest[:1])


def add16(a, b):
    return (a.astype(F32) + b.astype(F32)).astype(BF)


def all_sum(v, order):
    for b in order[:-1]:
        half = v.shape[0] // 2
        mine = bit_of(b)
        send = lax.dynamic_slice_in_dim(v, (1 - mine) * half, half, 0)
        keep = lax.dynamic_slice_in_dim(v, mine * half, half, 0)
        v = add16(keep, exchange(send, b))
    for b in order[-1:]:
        v = add16(v, exchange(v, b))
    for b in order[:-1][::-1]:
        other = exchange(v, b)
        v = jnp.where(
            bit_of(b) == 1,
            jnp.concatenate([other, v], 0),
            jnp.concatenate([v, other], 0),
        )
    return v


def group_sum(arrays):
    n = lax.axis_size("batch")
    if not is_power(n) or n == 1:
        return [lax.psum(a, "batch").astype(F32) for a in arrays]
    whole = jnp.concatenate(arrays, 0) if len(arrays) > 1 else arrays[0]
    half = whole.shape[0] // 2
    first, second = orders()
    whole = jnp.concatenate([all_sum(whole[:half], first), all_sum(whole[half:], second)], 0)
    out, at = [], 0
    for a in arrays:
        out.append(whole[at : at + a.shape[0]].astype(F32))
        at += a.shape[0]
    return out


def ffn_forward_kernel(x_ref, gain_ref, up_ref, down_ref, part_ref, pre_ref, u_ref, acc_ref):
    i = pl.program_id(0)
    rows = 256
    steps = x_ref.shape[0] // rows

    @pl.when(i == 0)
    def _():
        for t in range(steps):
            at = pl.ds(t * rows, rows)
            hat, _ = norm_parts(x_ref[at, :])
            u_ref[at, :] = (hat * gain_ref[...]).astype(BF)

    for t in range(steps):
        at = pl.ds(t * rows, rows)
        a = dot(u_ref[at, :], up_ref[...], 1, 1)
        pre_ref[at, :] = a.astype(BF)
        h = (a * jax.nn.sigmoid(a)).astype(BF)
        f = dot(h, down_ref[...])

        @pl.when(i == 0)
        def _():
            acc_ref[at, :] = f

        @pl.when(i > 0)
        def _():
            acc_ref[at, :] += f

    @pl.when(i == pl.num_programs(0) - 1)
    def _():
        part_ref[...] = acc_ref[...].astype(BF)


def whole_spec(shape):
    return pl.BlockSpec(shape, lambda *_: (0,) * len(shape))


def ffn_forward(x, gain, up, down):
    t, d = x.shape
    hid = up.shape[0]
    blk = min(512, hid)
    return pl.pallas_call(
        ffn_forward_kernel,
        grid=(hid // blk,),
        in_specs=[
            whole_spec((t, d)),
            whole_spec((1, d)),
            pl.BlockSpec((blk, d), lambda i: (i, 0)),
            pl.BlockSpec((blk, d), lambda i: (i, 0)),
        ],
        out_specs=[
            whole_spec((t, d)),
            pl.BlockSpec((t, blk), lambda i: (0, i)),
            whole_spec((t, d)),
        ],
        out_shape=[
            jax.ShapeDtypeStruct((t, d), BF),
            jax.ShapeDtypeStruct((t, hid), BF),
            jax.ShapeDtypeStruct((t, d), BF),
        ],
        scratch_shapes=[pltpu.VMEM((t, d), F32)],
        compiler_params=pltpu.CompilerParams(vmem_limit_bytes=VMEM),
        cost_estimate=pl.CostEstimate(
            flops=4 * t * d * hid, bytes_accessed=8 * t * d + 4 * hid * d, transcendentals=t * hid
        ),
        name="ffn_forward",
    )(x, gain[None], up, down)


def ffn_down_kernel(g_ref, pre_ref, out_ref, gf_ref):
    @pl.when(pl.program_id(0) == 0)
    def _():
        gf_ref[...] = (0.5 * g_ref[...]).astype(BF)

    a = pre_ref[...].astype(F32)
    h = (a * jax.nn.sigmoid(a)).astype(BF)
    out_ref[...] = dot(h, gf_ref[...], 0, 0).astype(BF)


def ffn_down_grad(g, pre):
    t, d = g.shape
    hid = pre.shape[1]
    blk = min(512, hid)
    return pl.pallas_call(
        ffn_down_kernel,
        grid=(hid // blk,),
        in_specs=[whole_spec((t, d)), pl.BlockSpec((t, blk), lambda i: (0, i))],
        out_specs=pl.BlockSpec((blk, d), lambda i: (i, 0)),
        out_shape=jax.ShapeDtypeStruct((hid, d), BF),
        scratch_shapes=[pltpu.VMEM((t, d), BF)],
        compiler_params=pltpu.CompilerParams(vmem_limit_bytes=VMEM),
        cost_estimate=pl.CostEstimate(
            flops=2 * t * d * hid, bytes_accessed=4 * t * d + 4 * hid * d, transcendentals=t * hid
        ),
        name="ffn_down_grad",
    )(g, pre)


def ffn_back_kernel(g_ref, pre_ref, u_ref, up_ref, down_ref, up_grad_ref, part_ref, gf_ref, acc_ref):
    i = pl.program_id(0)
    rows = 256
    steps = g_ref.shape[0] // rows

    @pl.when(i == 0)
    def _():
        gf_ref[...] = (0.5 * g_ref[...]).astype(BF)

    parts = []
    for t in range(steps):
        at = pl.ds(t * rows, rows)
        gh = dot(gf_ref[at, :], down_ref[...], 1, 1)
        ga = (gh * slope(pre_ref[at, :].astype(F32))).astype(BF)
        f = dot(ga, up_ref[...])

        @pl.when(i == 0)
        def _():
            acc_ref[at, :] = f

        @pl.when(i > 0)
        def _():
            acc_ref[at, :] += f

        parts.append(ga)
    ga = jnp.concatenate(parts, 0)
    up_grad_ref[...] = dot(ga, u_ref[...], 0, 0).astype(BF)

    @pl.when(i == pl.num_programs(0) - 1)
    def _():
        part_ref[...] = acc_ref[...].astype(BF)


def ffn_back(g, pre, u, up, down):
    t, d = g.shape
    hid = up.shape[0]
    blk = min(512, hid)
    return pl.pallas_call(
        ffn_back_kernel,
        grid=(hid // blk,),
        in_specs=[
            whole_spec((t, d)),
            pl.BlockSpec((t, blk), lambda i: (0, i)),
            whole_spec((t, d)),
            pl.BlockSpec((blk, d), lambda i: (i, 0)),
            pl.BlockSpec((blk, d), lambda i: (i, 0)),
        ],
        out_specs=[pl.BlockSpec((blk, d), lambda i: (i, 0)), whole_spec((t, d))],
        out_shape=[jax.ShapeDtypeStruct((hid, d), BF), jax.ShapeDtypeStruct((t, d), BF)],
        scratch_shapes=[pltpu.VMEM((t, d), BF), pltpu.VMEM((t, d), F32)],
        compiler_params=pltpu.CompilerParams(vmem_limit_bytes=VMEM),
        cost_estimate=pl.CostEstimate(
            flops=6 * t * d * hid, bytes_accessed=8 * t * d + 8 * hid * d, transcendentals=t * hid
        ),
        name="ffn_back",
    )(g, pre, u, up, down)


def turned(rows, length):
    return pl.ds(pl.multiple_of(lax.rem(length - pl.program_id(1) * rows, length), rows), length)


def fill_twice(twice_ref, pos_ref):
    length = pos_ref.shape[0]

    @pl.when(pl.program_id(1) == 0)
    def _():
        twice_ref[:length, :] = pos_ref[...]
        twice_ref[length:, :] = pos_ref[...]


def masked_scores(segq_ref, segk_ref, qc_ref, qp_ref, k_ref, pos):
    far = pltpu.roll(dot(qp_ref[...], pos, 1, 1), 0, 1, stride=1, stride_axis=0)
    z = dot(qc_ref[...], k_ref[...], 1, 1) + far
    z = jnp.where(segq_ref[...] == segk_ref[...], z, NEG)
    e = jnp.exp2((z - jnp.max(z, axis=1, keepdims=True)) * (math.log2(math.e) / math.sqrt(DH)))
    return e, 1.0 / jnp.sum(e, axis=1, keepdims=True)


def attention_kernel(segq_ref, segk_ref, qc_ref, qp_ref, k_ref, v_ref, pos_ref, out_ref, twice_ref):
    fill_twice(twice_ref, pos_ref)
    pos = twice_ref[turned(qc_ref.shape[0], k_ref.shape[0]), :]
    e, inverse = masked_scores(segq_ref, segk_ref, qc_ref, qp_ref, k_ref, pos)
    out_ref[...] = (dot(e.astype(BF), v_ref[...]) * inverse).astype(BF)


def attention_specs(t, rows):
    by_query = pl.BlockSpec((rows, DH), lambda h, i: (i, h))
    by_head = pl.BlockSpec((t, DH), lambda h, i: (0, h))
    return by_query, by_head, [
        pl.BlockSpec((rows, 1), lambda h, i: (i, 0)),
        pl.BlockSpec((1, t), lambda h, i: (0, 0)),
    ]


def attention(seg, qc, qp, k, v, pos):
    t, width = qc.shape
    heads = width // DH
    rows = min(256, t)
    by_query, by_head, seg_specs = attention_specs(t, rows)
    return pl.pallas_call(
        attention_kernel,
        grid=(heads, t // rows),
        in_specs=seg_specs + [by_query, by_query, by_head, by_head, by_head],
        out_specs=by_query,
        out_shape=jax.ShapeDtypeStruct((t, width), BF),
        scratch_shapes=[pltpu.VMEM((2 * t, DH), BF)],
        compiler_params=pltpu.CompilerParams(vmem_limit_bytes=VMEM),
        cost_estimate=pl.CostEstimate(
            flops=12 * t * t * width, bytes_accessed=12 * t * width, transcendentals=heads * t * t
        ),
        name="attention_forward",
    )(seg[:, None], seg[None, :], qc, qp, k, v, pos)


def attention_back_kernel(
    segq_ref, segk_ref, qc_ref, qp_ref, k_ref, v_ref, pos_ref, gctx_ref,
    gq_ref, gk_ref, gv_ref, gpos_ref, content_ref, position_ref, gk_acc, gv_acc, twice_ref, gpos_acc,
):
    i = pl.program_id(1)
    rows = qc_ref.shape[0]
    length = k_ref.shape[0]

    @pl.when(i == 0)
    def _():
        gk_acc[...] = jnp.zeros_like(gk_acc)
        gv_acc[...] = jnp.zeros_like(gv_acc)
        gpos_acc[...] = jnp.zeros_like(gpos_acc)
        content_ref[...] = jnp.zeros_like(content_ref)
        position_ref[...] = jnp.zeros_like(position_ref)

    fill_twice(twice_ref, pos_ref)
    place = turned(rows, length)
    pos = twice_ref[place, :]
    e, inverse = masked_scores(segq_ref, segk_ref, qc_ref, qp_ref, k_ref, pos)
    prob = e * inverse
    gctx = gctx_ref[...]
    gprob = dot(gctx, v_ref[...], 1, 1)
    gv_acc[...] += dot(prob.astype(BF), gctx, 0, 0)
    inner = jnp.sum(prob * gprob, axis=1, keepdims=True)
    gz = (prob * (gprob - inner) * (1.0 / math.sqrt(DH))).astype(BF)
    gqc = dot(gz, k_ref[...])
    gk_acc[...] += dot(gz, qc_ref[...], 0, 0)
    at_row = lax.broadcasted_iota(jnp.int32, (rows, rows), 0)
    at_col = lax.broadcasted_iota(jnp.int32, (rows, rows), 1)
    flip = jnp.where(at_row + at_col == rows - 1, 1.0, 0.0).astype(BF)
    wide = pltpu.roll(dot(flip, gz), length - rows + 1, 1, stride=1, stride_axis=0).astype(BF)
    qp_flip = dot(flip, qp_ref[...]).astype(BF)
    gqp = dot(wide, pos)
    gpos_acc[place, :] += dot(wide, qp_flip, 0, 0)
    gq_ref[...] = (gqc + dot(flip, gqp.astype(BF))).astype(BF)
    content_ref[0] += jnp.sum(gqc, axis=0, keepdims=True)
    position_ref[0] += jnp.sum(gqp, axis=0, keepdims=True)

    @pl.when(i == pl.num_programs(1) - 1)
    def _():
        gk_ref[...] = gk_acc[...].astype(BF)
        gv_ref[...] = gv_acc[...].astype(BF)
        gpos_ref[...] = gpos_acc[:length, :] + gpos_acc[length:, :]


def attention_back(seg, qc, qp, k, v, pos, gctx):
    t, width = qc.shape
    heads = width // DH
    rows = min(256, t)
    by_query, by_head, seg_specs = attention_specs(t, rows)
    bias = pl.BlockSpec((1, 1, DH), lambda h, i: (h, 0, 0))
    return pl.pallas_call(
        attention_back_kernel,
        grid=(heads, t // rows),
        in_specs=seg_specs + [by_query, by_query, by_head, by_head, by_head, by_query],
        out_specs=[by_query, by_head, by_head, by_head, bias, bias],
        out_shape=[
            jax.ShapeDtypeStruct((t, width), BF),
            jax.ShapeDtypeStruct((t, width), BF),
            jax.ShapeDtypeStruct((t, width), BF),
            jax.ShapeDtypeStruct((t, width), F32),
            jax.ShapeDtypeStruct((heads, 1, DH), F32),
            jax.ShapeDtypeStruct((heads, 1, DH), F32),
        ],
        scratch_shapes=[
            pltpu.VMEM((t, DH), F32),
            pltpu.VMEM((t, DH), F32),
            pltpu.VMEM((2 * t, DH), BF),
            pltpu.VMEM((2 * t, DH), F32),
        ],
        compiler_params=pltpu.CompilerParams(vmem_limit_bytes=VMEM),
        cost_estimate=pl.CostEstimate(
            flops=36 * t * t * width, bytes_accessed=24 * t * width, transcendentals=heads * t * t
        ),
        name="attention_back",
    )(seg[:, None], seg[None, :], qc, qp, k, v, pos, gctx)


def encoding(length, features):
    half = features // 2
    frequency = jnp.exp(jnp.arange(half).astype(F32) * (-2.0 * math.log(10000.0) / features))
    fine = 32
    steps = jnp.arange(length // fine) * fine
    a = jnp.where(steps < length // 2, -steps, length - steps).astype(F32)[:, None] * frequency[None]
    b = jnp.arange(fine).astype(F32)[:, None] * frequency[None]
    sa, ca = jnp.sin(a)[:, None], jnp.cos(a)[:, None]
    sb, cb = jnp.sin(b)[None], jnp.cos(b)[None]
    sine = sa * cb - ca * sb
    cosine = ca * cb + sa * sb
    return jnp.concatenate([sine, cosine], axis=-1).reshape(length, features).astype(BF)


def on_device(
    frames,
    segment_ids,
    valid_mask,
    first_norm,
    first_up,
    first_down,
    attention_norm,
    query_proj,
    key_proj,
    value_proj,
    output_proj,
    position_proj,
    content_bias,
    position_bias,
    convolution_norm,
    pointwise_in,
    depthwise,
    batch_gain,
    batch_shift,
    pointwise_out,
    second_norm,
    second_up,
    second_down,
    final_norm,
    cotangent,
):
    groups = lax.axis_size("fsdp")
    member = lax.axis_index("fsdp")
    shard_frames, d = frames.shape[1:]
    t = segment_ids.shape[1]
    part = d // groups
    seg = segment_ids[0]
    valid = valid_mask[0].astype(F32)[:, None]

    def own(v, axis=0):
        return lax.dynamic_slice_in_dim(v, member * part, part, axis)

    x0 = gather_rows(frames[0]).astype(F32)
    cot = gather_rows(cotangent[0]).astype(F32)
    value_in, gate_in = pointwise_in[:, :d], pointwise_in[:, d:]
    columns = own_columns(
        [(m, part) for m in (query_proj, key_proj, value_proj, value_in, gate_in, position_proj)]
    )
    qkv_own = columns[:, : 3 * part]
    in_own = columns[:, 3 * part : 5 * part]
    pos_own = columns[:, 5 * part :]
    encoded = encoding(t, d)
    pos = dot(encoded, pos_own).astype(BF)

    part_sum, pre1, u1 = ffn_forward(x0, first_norm, first_up, first_down)
    x1 = x0 + 0.5 * pair_sum(part_sum)
    hat, _ = norm_parts(x1)
    ua = (hat * attention_norm).astype(BF)
    qkv = dot(ua, qkv_own)
    queries = qkv[:, :part]
    keys = qkv[:, part : 2 * part].astype(BF)
    values = qkv[:, 2 * part :].astype(BF)
    qc = (queries + own(content_bias)).astype(BF)
    qp = (queries + own(position_bias)).astype(BF)
    ctx = attention(seg, qc, qp, keys, values, pos)
    x2 = x1 + pair_sum(dot(ctx, output_proj).astype(BF))
    hat, _ = norm_parts(x2)
    uc = (hat * convolution_norm).astype(BF)
    gp = dot(uc, in_own)
    signal, opener = gp[:, :part], jax.nn.sigmoid(gp[:, part:])
    glu = signal * opener
    taps = own(depthwise)
    seg_rim = jnp.pad(seg, (RIM, RIM), constant_values=-1)
    linked = [(seg_rim[o : o + t] == seg).astype(F32)[:, None] for o in range(KER)]

    def rims(v):
        return jnp.pad(v, ((RIM, RIM), (0, 0)))

    glu_rim = rims(glu)
    dc = sum(glu_rim[o : o + t] * linked[o] * taps[:, o] for o in range(KER))
    weighted = valid * dc
    sums = jnp.stack(
        [
            jnp.sum(weighted, axis=0),
            jnp.sum(weighted * dc, axis=0),
            jnp.full((part,), jnp.sum(valid)),
        ]
    )
    sums = row_sum(sums)
    count = sums[2]
    mu = sums[0] / count
    brstd = lax.rsqrt(sums[1] / count - mu * mu + EPS)
    gain_own, shift_own = own(batch_gain), own(batch_shift)

    def standard():
        return (dc - mu) * brstd

    bo = standard() * gain_own + shift_own
    sw = jax.nn.silu(bo).astype(BF)
    x3 = x2 + pair_sum(dot(sw, pointwise_out).astype(BF))
    part_sum, pre2, u2 = ffn_forward(x3, second_norm, second_up, second_down)
    x4 = x3 + 0.5 * pair_sum(part_sum)
    hat, rstd = norm_parts(x4)
    layer_out = lax.dynamic_slice_in_dim(hat, member * shard_frames, shard_frames, 0)
    layer_out = (layer_out * final_norm).astype(BF)[None]

    final_gain = jnp.sum(cot * hat, axis=0)
    g = norm_back(cot, hat, rstd, final_norm)
    second_down_grad = ffn_down_grad(g, pre2)
    second_up_grad, part_sum = ffn_back(g, pre2, u2, second_up, second_down)
    second_sum = group_sum([second_down_grad, second_up_grad])
    gu = pair_sum(part_sum)
    hat, rstd = norm_parts(x3)
    second_gain = jnp.sum(gu * hat, axis=0)
    g = g + norm_back(gu, hat, rstd, second_norm)

    gco = g.astype(BF)
    out_w_grad = dot(sw, gco, 0, 0).astype(BF)
    gbo = dot(gco, pointwise_out, 1, 1) * slope(bo)
    ab = row_sum(jnp.stack([jnp.sum(gbo, axis=0), jnp.sum(gbo * standard(), axis=0)]))
    gmu = -brstd * gain_own * ab[0]
    gvar = -0.5 * brstd * brstd * gain_own * ab[1]
    gdc = gbo * (gain_own * brstd) + valid * ((gmu - 2.0 * mu * gvar + 2.0 * dc * gvar) / count)
    gdc_rim = rims(gdc)
    gglu = sum(
        gdc_rim[KER - 1 - o : KER - 1 - o + t] * linked[KER - 1 - o] * taps[:, o]
        for o in range(KER)
    )
    taps_grad = [jnp.sum(gdc * glu_rim[o : o + t] * linked[o], axis=0) for o in range(KER)]
    ggp = jnp.concatenate([gglu * opener, gglu * signal * opener * (1.0 - opener)], axis=1)
    ggp = ggp.astype(BF)
    in_w_grad = dot(uc, ggp, 0, 0).astype(BF)
    gu = pair_sum(dot(ggp, in_own, 1, 1).astype(BF))
    hat, rstd = norm_parts(x2)
    conv_gain = jnp.sum(gu * hat, axis=0)
    g = g + norm_back(gu, hat, rstd, convolution_norm)

    gao = g.astype(BF)
    output_grad = dot(ctx, gao, 0, 0).astype(BF)
    gctx = dot(gao, output_proj, 1, 1).astype(BF)
    gq, gk, gv, gpos, content_grad, position_grad = attention_back(
        seg, qc, qp, keys, values, pos, gctx
    )
    gqkv = jnp.concatenate([gq, gk, gv], axis=1)
    qkv_grad = dot(ua, gqkv, 0, 0).astype(BF)
    gpos_high = gpos.astype(BF)
    gpos_low = (gpos - gpos_high.astype(F32)).astype(BF)
    pos_grad = (dot(encoded, gpos_high, 0, 0) + dot(encoded, gpos_low, 0, 0)).astype(BF)
    gu = pair_sum(dot(gqkv, qkv_own, 1, 1).astype(BF))
    hat, rstd = norm_parts(x1)
    attention_gain = jnp.sum(gu * hat, axis=0)
    g = g + norm_back(gu, hat, rstd, attention_norm)

    swapped = row_blocks_swap(jnp.concatenate([qkv_grad, in_w_grad, pos_grad], axis=1))

    def unfold(at):
        block = swapped[:, :, at * part : (at + 1) * part]
        return jnp.swapaxes(block, 0, 1).reshape(part, d)

    middle_sum = group_sum([out_w_grad, output_grad] + [unfold(at) for at in range(6)])

    first_down_grad = ffn_down_grad(g, pre1)
    first_up_grad, part_sum = ffn_back(g, pre1, u1, first_up, first_down)
    first_sum = group_sum([first_down_grad, first_up_grad])
    gu = pair_sum(part_sum)
    hat, rstd = norm_parts(x0)
    first_gain = jnp.sum(gu * hat, axis=0)
    g = g + norm_back(gu, hat, rstd, first_norm)
    frames_grad = lax.dynamic_slice_in_dim(g, member * shard_frames, shard_frames, 0)
    frames_grad = frames_grad.astype(BF)[None]

    gains = [own(v) for v in (first_gain, attention_gain, conv_gain, second_gain, final_gain)]
    small = jnp.stack(
        gains + [content_grad.reshape(part), position_grad.reshape(part)] + taps_grad
    )
    small = row_sum(small)
    out_w_grad, output_grad, q_grad, k_grad, v_grad, value_grad, gate_grad, pos_grad = middle_sum
    return (
        layer_out,
        frames_grad,
        small[0],
        first_sum[1],
        first_sum[0],
        small[1],
        q_grad,
        k_grad,
        v_grad,
        output_grad,
        pos_grad,
        small[5],
        small[6],
        small[2],
        jnp.concatenate([value_grad, gate_grad], axis=1),
        small[7:].T,
        ab[1],
        ab[0],
        out_w_grad,
        small[3],
        second_sum[1],
        second_sum[0],
        small[4],
    )


def solution(mesh):
    rows, shard, whole = P("batch", "fsdp", None), P("fsdp", None), P()
    return jax.shard_map(
        on_device,
        mesh=mesh,
        in_specs=(
            rows,
            P("batch", None),
            P("batch", None),
            whole,
            shard,
            shard,
            whole,
            shard,
            shard,
            shard,
            shard,
            shard,
            whole,
            whole,
            whole,
            shard,
            whole,
            whole,
            whole,
            shard,
            whole,
            shard,
            shard,
            whole,
            rows,
        ),
        out_specs=(
            rows,
            rows,
            P("fsdp"),
            shard,
            shard,
            P("fsdp"),
            shard,
            shard,
            shard,
            shard,
            shard,
            P("fsdp"),
            P("fsdp"),
            P("fsdp"),
            shard,
            shard,
            P("fsdp"),
            P("fsdp"),
            shard,
            P("fsdp"),
            shard,
            shard,
            P("fsdp"),
        ),
        check_vma=False,
    )
```

```python
import functools
import math

import jax
import jax.numpy as jnp
from jax import lax
from jax.experimental import pallas as pl
from jax.experimental.pallas import tpu as pltpu
from jax.sharding import PartitionSpec as P

H = 8
DH = 128
KER = 5
RIM = (KER - 1) // 2
EPS = 1e-05
NEG = -1e30
BF = jnp.bfloat16
F32 = jnp.float32
VMEM = 56 * 1024 * 1024
PLAN = ("", "a", "", "a", "a", "", "ba", "a", "bcab", "c", "b", "cdbac", "dc", "bedc", "eedb", "feescfdscfesdfesfdfsdf")


def dot(a, b, da=1, db=0):
    return lax.dot_general(a, b, (((da,), (db,)), ((), ())), preferred_element_type=F32)


def norm_parts(v):
    centred = v - jnp.mean(v, axis=-1, keepdims=True)
    rstd = lax.rsqrt(jnp.mean(centred * centred, axis=-1, keepdims=True) + EPS)
    return centred * rstd, rstd


def norm_back(grad, hat, rstd, gain):
    scaled = grad * gain
    first = jnp.mean(scaled, axis=-1, keepdims=True)
    second = jnp.mean(scaled * hat, axis=-1, keepdims=True)
    return rstd * (scaled - first - hat * second)


def slope(v):
    s = jax.nn.sigmoid(v)
    return s * (1.0 + v * (1.0 - s))


def shifted(v, s):
    g = lax.axis_size("fsdp")
    return lax.ppermute(v, "fsdp", [(i, (i + s) % g) for i in range(g)])


def natural(blocks):
    g = len(blocks)
    me = lax.axis_index("fsdp")
    if g == 1:
        return blocks[0][None]
    if g == 2:
        a, b = blocks
        return jnp.where(me == 0, jnp.stack([a, b]), jnp.stack([b, a]))
    stacked = jnp.stack(blocks[::-1])
    return jnp.roll(stacked, me + 1, axis=0)


def gather_rows(v, place):
    g = lax.axis_size("fsdp")
    if g == 2:
        return placed(place, v, shifted(v, 1))
    out = natural([v] + [shifted(v, s) for s in range(1, g)])
    return out.reshape((g * v.shape[0],) + v.shape[1:])


def pair_swap(v):
    g = lax.axis_size("fsdp")
    if g == 2:
        return lax.all_to_all(v, "fsdp", 0, 0)
    other = pair_other(v[0])
    return jnp.stack([other, other])


def pair_other(v):
    g = lax.axis_size("fsdp")
    if g == 2:
        return shifted(v, 1)
    return sum(shifted(v, s).astype(F32) for s in range(1, g))


def row_blocks_swap(v):
    g = lax.axis_size("fsdp")
    n = v.shape[0] // g
    return lax.all_to_all(v.reshape(g, n, v.shape[1]), "fsdp", 0, 0)


def own_columns(matrices):
    g = lax.axis_size("fsdp")
    me = lax.axis_index("fsdp")

    def columns(member):
        parts = []
        for m, width in matrices:
            parts.append(lax.dynamic_slice_in_dim(m, member * width, width, 1))
        return jnp.concatenate(parts, axis=1)

    blocks = [columns(me)]
    for s in range(1, g):
        blocks.append(shifted(columns(lax.rem(me + s, g)), s))
    return blocks


def bit_of(b):
    return (lax.axis_index("batch") >> b) & 1


def exchange(v, b):
    n = lax.axis_size("batch")
    return lax.ppermute(v, "batch", [(i, i ^ (1 << b)) for i in range(n)])


def is_power(n):
    return n & (n - 1) == 0


def row_sum(v):
    n = lax.axis_size("batch")
    if not is_power(n):
        return lax.psum(v, "batch")
    for b in range(n.bit_length() - 1):
        v = v + exchange(v, b)
    return v


def add16(a, b):
    return (a.astype(F32) + b.astype(F32)).astype(BF)


def halves(v, b):
    half = v.shape[0] // 2
    mine = bit_of(b)
    keep = lax.dynamic_slice_in_dim(v, mine * half, half, 0)
    return keep, lax.dynamic_slice_in_dim(v, (1 - mine) * half, half, 0)


def joined(v, other, b):
    low, high = jnp.concatenate([v, other], 0), jnp.concatenate([other, v], 0)
    return jnp.where(bit_of(b) == 1, high, low)


class Sequence:
    def __init__(self):
        self.last = None

    def run(self, step, *inputs):
        if self.last is not None:
            *inputs, _ = lax.optimization_barrier((*inputs, self.last))
        outputs = step(*inputs)
        leaves = jax.tree.leaves(outputs)
        self.last = leaves[0] if leaves else self.last
        return outputs


    def tie(self, *values):
        if self.last is None:
            return values
        return lax.optimization_barrier((*values, self.last))[:-1]


class BatchSum:
    def __init__(self, sequence, arrays, parts=None):
        self.sequence = sequence
        self.parts = parts
        self.sizes = arrays if parts is not None else [a.shape[0] for a in arrays]
        self.arrays = arrays
        bits = lax.axis_size("batch").bit_length() - 1
        rest = list(range(3, bits))
        self.bits = list(zip([0, 2, 1] + rest, [1, 2, 0] + rest, strict=True))
        self.event = 0
        self.out = None

    def send(self, k, pair):
        a, b = self.bits[k]
        if a == b:
            got = exchange(pair, a)
            return got[0], got[1]
        return exchange(pair[0], a), exchange(pair[1], b)

    def launch(self, k, now):
        a, b = self.bits[k]
        parts = [halves(now[0], a), halves(now[1], b)]
        keep, away = tuple(p[0] for p in parts), tuple(p[1] for p in parts)
        return keep, (jnp.stack(away) if a == b else away)

    def step(self):
        e, n = self.event, len(self.bits)
        self.event += 1
        if e == 0 and self.parts is not None:
            self.keep, away = self.parts
            self.got = self.send(0, away)
        elif e == 0:

            def first(*arrays):
                whole = jnp.concatenate(arrays, 0) if len(arrays) > 1 else arrays[0]
                half = whole.shape[0] // 2
                return self.launch(0, (whole[:half], whole[half:]))

            self.keep, away = self.sequence.run(first, *self.arrays)
            self.got = self.send(0, away)
        elif e < n:

            def add(k0, k1, g0, g1):
                now = (add16(k0, g0), add16(k1, g1))
                if e < n - 1:
                    return self.launch(e, now)
                return (jnp.stack(now),)

            out = self.sequence.run(add, *self.keep, *self.got)
            if e < n - 1:
                self.keep, away = out
                self.got = self.send(e, away)
            else:
                self.keep = out[0]
                self.got = exchange(self.keep, self.bits[e][0])
        elif e == n:

            def last(k, g):
                now = add16(k, g)
                return self.spread(n - 2, (now[0], now[1]))

            now = self.sequence.run(last, self.keep, self.got)
            self.forward(n - 2, now)
        elif e < 2 * n - 1:
            k = 2 * n - 2 - e

            def more(c0, c1, g0, g1):
                a, b = self.bits[k + 1]
                return self.spread(k, (joined(c0, g0, a), joined(c1, g1, b)))

            now = self.sequence.run(more, *self.now, *self.got)
            self.forward(k, now)
        else:

            def final(c0, c1, g0, g1):
                a, b = self.bits[0]
                whole = jnp.concatenate([joined(c0, g0, a), joined(c1, g1, b)], 0)
                out, at = [], 0
                for size in self.sizes:
                    out.append(whole[at : at + size].astype(F32))
                    at += size
                return out

            self.out = self.sequence.run(final, *self.now, *self.got)

    def spread(self, k, now):
        a, b = self.bits[k]
        return jnp.stack(now) if a == b else now

    def forward(self, k, now):
        self.now = (now[0], now[1])
        self.got = self.send(k, now)

    def finish(self):
        while self.out is None:
            self.step()
        return self.out


class SmallSum:
    def __init__(self, sequence, v):
        self.sequence = sequence
        self.v = v
        self.bit = 0
        self.got = exchange(v, 0)
        self.bits = lax.axis_size("batch").bit_length() - 1

    def step(self):
        if self.bit == self.bits:
            return
        self.v = self.sequence.run(lambda a, b: a + b, self.v, self.got)
        self.bit += 1
        if self.bit < self.bits:
            self.got = exchange(self.v, self.bit)

    def finish(self):
        while self.bit < self.bits:
            self.step()
        return self.v


ROWS = 256
CHEAP = pl.CostEstimate(flops=1, bytes_accessed=1, transcendentals=0)


def launch(kernel, name, steps, place, ins, outs, scratch=()):
    return pl.pallas_call(
        kernel,
        grid_spec=pltpu.PrefetchScalarGridSpec(
            num_scalar_prefetch=1,
            grid=(steps,),
            in_specs=[spec for _, spec in ins],
            out_specs=[spec for _, _, spec in outs],
            scratch_shapes=list(scratch),
        ),
        out_shape=[jax.ShapeDtypeStruct(shape, kind) for shape, kind, _ in outs],
        compiler_params=pltpu.CompilerParams(vmem_limit_bytes=VMEM),
        cost_estimate=CHEAP,
        name=name,
    )(place, *[a for a, _ in ins])


def whole(shape):
    return pl.BlockSpec(tuple(shape), lambda i, place: (0,) * len(shape))


def all_of(a):
    return a, whole(a.shape)


def blocks_of(shape, lag=0):
    last = shape[0] // ROWS - 1
    return pl.BlockSpec((ROWS, shape[1]), lambda i, place: (jnp.clip(i - lag, 0, last), 0))


def by_rows(a, lag=0):
    return a, blocks_of(a.shape, lag)


def out_rows(shape, kind, lag=0):
    return shape, kind, blocks_of(shape, lag)


def out_twice(shape, kind, lag=0):
    last = shape[0] // ROWS - 1
    spec = pl.BlockSpec((2, ROWS, shape[1]), lambda i, place: (0, jnp.clip(i - lag, 0, last), 0))
    return (2, *shape), kind, spec


def two_parts(part, other):
    last = part.shape[1] // ROWS - 1
    block = (None, ROWS, part.shape[2])
    return [
        (part, pl.BlockSpec(block, lambda i, place: (0, jnp.minimum(i, last), 0))),
        (other, pl.BlockSpec(block, lambda i, place: (place[0], jnp.minimum(i, last), 0))),
    ]


def out_all(shape, kind):
    return shape, kind, whole(shape)


def columns_of(place, s, width):
    return pl.ds(pl.multiple_of(place[8 + s] * width, width), width)


def first_step(*refs):
    @pl.when(pl.program_id(0) == 0)
    def _():
        for ref in refs:
            ref[...] = jnp.zeros_like(ref)


def last_step():
    return pl.program_id(0) == pl.num_programs(0) - 1


def wide(*refs):
    return [ref[...].astype(F32) for ref in refs]


def placed_kernel(place, own, other, out):
    @pl.when(pl.program_id(0) == 0)
    def _():
        out[...] = own[...]

    @pl.when(pl.program_id(0) == 1)
    def _():
        out[...] = other[...]


def placed(place, own, other):
    n, d = own.shape
    spec = pl.BlockSpec((n, d), lambda i, place: ((place[0] + 1 + i) % 2, 0))
    ins, outs = [all_of(own), all_of(other)], [((2 * n, d), own.dtype, spec)]
    return launch(placed_kernel, "placed", 2, place, ins, outs)[0]


def pack_kernel(place, *refs):
    half = len(refs) // 2 - 1
    own, away = refs[-2:]
    width = refs[0].shape[1]
    for j in range(half):
        columns = slice(j * width, (j + 1) * width)
        own[:, columns] = refs[j][...]
        away[:, columns] = refs[half + j][...]


def packed(place, matrices):
    n = matrices[0][0].shape[0]
    width = matrices[0][2]

    def part(m, first, mine):
        def at(i, place):
            member = (place[0] + 1) % 2 if mine else place[0]
            return (0, first + member)

        return m, pl.BlockSpec((n, width), at)

    ins = [part(m, first, mine) for mine in (True, False) for m, first, _ in matrices]
    outs = [((n, len(matrices) * width), BF, whole((n, len(matrices) * width)))] * 2
    return launch(pack_kernel, "packed", 1, place, ins, outs)


def ffn_forward_kernel(place, *refs, joined):
    if joined:
        base, p, r, gain, up, down, x_ref, part, pre, u_ref = refs
        a, b, c = wide(base, p, r)
        x = a + (b + c)
        x_ref[...] = x
    else:
        base, gain, up, down, part, pre, u_ref = refs
        (x,) = wide(base)
    u = (norm_parts(x)[0] * gain[...]).astype(BF)
    u_ref[...] = u
    chunk = min(1024, up.shape[0])
    total = None
    for c in range(0, up.shape[0], chunk):
        a = dot(u, up[c : c + chunk, :], 1, 1)
        pre[:, c : c + chunk] = a.astype(BF)
        h = (a * jax.nn.sigmoid(a)).astype(BF)
        f = dot(h, down[c : c + chunk, :])
        total = f if total is None else total + f
    part[...] = total.astype(BF)


def ffn_forward(place, base, pair, gain, up, down):
    t, d = base.shape
    hid = up.shape[0]
    ins = [by_rows(base)] + [by_rows(v) for v in pair] + [all_of(gain[None]), all_of(up), all_of(down)]
    outs = [out_rows((t, d), BF), out_rows((t, hid), BF), out_rows((t, d), BF)]
    if pair:
        outs = [out_rows((t, d), F32)] + outs
    kernel = functools.partial(ffn_forward_kernel, joined=bool(pair))
    return launch(kernel, "ffn_forward", t // ROWS, place, ins, outs)


def qkv_kernel(place, base, p, r, gain, content, position, *refs, groups):
    blocks, (x_ref, ua, qc, qp, k, v) = refs[:groups], refs[groups:]
    a, b, c = wide(base, p, r)
    x = a + 0.5 * (b + c)
    x_ref[...] = x
    ua[...] = (norm_parts(x)[0] * gain[...]).astype(BF)
    n = blocks[0].shape[0]
    all3 = sum(dot(ua[:, columns_of(place, s, n)], w[...]) for s, w in enumerate(blocks))
    part = qc.shape[1]
    q = all3[:, :part]
    qc[...] = (q + content[...]).astype(BF)
    qp[...] = (q + position[...]).astype(BF)
    k[...] = all3[:, part : 2 * part].astype(BF)
    v[...] = all3[:, 2 * part :].astype(BF)


def weight_blocks(blocks, width, at):
    return [(w, pl.BlockSpec((w.shape[0], width), lambda i, place: (0, at))) for w in blocks]


def qkv_forward(place, base, p, r, gain, content, position, blocks):
    t, d = base.shape
    part = content.shape[0]
    ins = [by_rows(base), by_rows(p), by_rows(r)]
    ins += [all_of(v[None]) for v in (gain, content, position)] + weight_blocks(blocks, 3 * part, 1)
    outs = [out_rows((t, d), F32), out_rows((t, d), BF)] + [out_rows((t, part), BF)] * 4
    kernel = functools.partial(qkv_kernel, groups=len(blocks))
    return launch(kernel, "qkv", t // ROWS, place, ins, outs)


def turned(rows, length):
    return pl.ds(pl.multiple_of(lax.rem(length - pl.program_id(0) * rows, length), rows), length)


def fill_twice(twice_ref, pos_ref):
    length = pos_ref.shape[0]

    @pl.when(pl.program_id(0) == 0)
    def _():
        twice_ref[:length, :] = pos_ref[...]
        twice_ref[length:, :] = pos_ref[...]


def exponentials(same, qc, qp, k, pos):
    far = pltpu.roll(dot(qp, pos, 1, 1), 0, 1, stride=1, stride_axis=0)
    z = jnp.where(same, dot(qc, k, 1, 1) + far, NEG)
    e = jnp.exp2((z - jnp.max(z, axis=1, keepdims=True)) * (math.log2(math.e) / math.sqrt(DH)))
    return e, 1.0 / jnp.sum(e, axis=1, keepdims=True)


def attention_kernel(place, segq, segk, qc, qp, k, v, pos, out_w, ctx, part, twice):
    fill_twice(twice, pos)
    at = turned(qc.shape[0], k.shape[0])
    same = segq[...] == segk[...]
    for h in range(qc.shape[1] // DH):
        c = slice(h * DH, (h + 1) * DH)
        e, inverse = exponentials(same, qc[:, c], qp[:, c], k[:, c], twice[at, c])
        ctx[:, c] = (dot(e.astype(BF), v[:, c]) * inverse).astype(BF)
    part[...] = dot(ctx[...], out_w[...]).astype(BF)


def attention(place, seg, qc, qp, k, v, pos, out_w):
    t, width = qc.shape
    d = out_w.shape[1]
    ins = [by_rows(seg[:, None]), all_of(seg[None]), by_rows(qc), by_rows(qp)]
    ins += [all_of(a) for a in (k, v, pos, out_w)]
    outs = [out_rows((t, width), BF), out_rows((t, d), BF)]
    scratch = [pltpu.VMEM((2 * t, width), BF)]
    return launch(attention_kernel, "attention_forward", t // ROWS, place, ins, outs, scratch)


def attention_back_kernel(
    place, segq, segk, qc, qp, k, v, pos, gctx,
    gq, gk, gv, gpos, content, position, gk_acc, gv_acc, twice, gpos_acc,
):
    rows, length = qc.shape[0], k.shape[0]
    first_step(gk_acc, gv_acc, gpos_acc, content, position)
    fill_twice(twice, pos)
    at = turned(rows, length)
    same = segq[...] == segk[...]
    at_row = lax.broadcasted_iota(jnp.int32, (rows, rows), 0)
    at_col = lax.broadcasted_iota(jnp.int32, (rows, rows), 1)
    flip = jnp.where(at_row + at_col == rows - 1, 1.0, 0.0).astype(BF)
    for h in range(qc.shape[1] // DH):
        c = slice(h * DH, (h + 1) * DH)
        near = twice[at, c]
        e, inverse = exponentials(same, qc[:, c], qp[:, c], k[:, c], near)
        prob = e * inverse
        gout = gctx[:, c]
        gprob = dot(gout, v[:, c], 1, 1)
        gv_acc[:, c] += dot(prob.astype(BF), gout, 0, 0)
        inner = jnp.sum(prob * gprob, axis=1, keepdims=True)
        gz = (prob * (gprob - inner) * (1.0 / math.sqrt(DH))).astype(BF)
        gqc = dot(gz, k[:, c])
        gk_acc[:, c] += dot(gz, qc[:, c], 0, 0)
        skew = pltpu.roll(dot(flip, gz), length - rows + 1, 1, stride=1, stride_axis=0).astype(BF)
        gqp = dot(skew, near)
        gpos_acc[at, c] += dot(skew, dot(flip, qp[:, c]).astype(BF), 0, 0)
        gq[:, c] = (gqc + dot(flip, gqp.astype(BF))).astype(BF)
        content[:, c] += jnp.sum(gqc, axis=0, keepdims=True)
        position[:, c] += jnp.sum(gqp, axis=0, keepdims=True)

    @pl.when(last_step())
    def _():
        gk[...] = gk_acc[...].astype(BF)
        gv[...] = gv_acc[...].astype(BF)
        gpos[...] = gpos_acc[:length, :] + gpos_acc[length:, :]


def attention_back(place, seg, qc, qp, k, v, pos, gctx, first):
    t, width = qc.shape
    if (width // DH) % 2 == 0:
        width //= 2
    elif not first:
        return None
    at = 0 if first else 1

    def columns(a, rows):
        return a, pl.BlockSpec((rows, width), lambda i, place: (i if rows < t else 0, at))

    ins = [by_rows(seg[:, None]), all_of(seg[None]), columns(qc, ROWS), columns(qp, ROWS)]
    ins += [columns(a, t) for a in (k, v, pos)] + [columns(gctx, ROWS)]
    outs = [out_rows((t, width), BF), out_all((t, width), BF), out_all((t, width), BF)]
    outs += [out_all((t, width), F32), out_all((1, width), F32), out_all((1, width), F32)]
    scratch = [pltpu.VMEM((t, width), F32)] * 2
    scratch += [pltpu.VMEM((2 * t, width), BF), pltpu.VMEM((2 * t, width), F32)]
    return launch(attention_back_kernel, "attention_back", t // ROWS, place, ins, outs, scratch)


EDGE = 8


def window(ref, block):
    return ref[pl.ds(pl.multiple_of(block * ROWS, ROWS), ROWS + 2 * EDGE), :]


def taken(rows, o):
    return rows[EDGE - RIM + o : EDGE - RIM + o + ROWS, :]


def keep_block(ref, block, rows):
    ref[pl.ds(pl.multiple_of(block * ROWS + EDGE, EDGE), ROWS), :] = rows


def clear_edges(*refs):
    @pl.when(pl.program_id(0) == 0)
    def _():
        for ref in refs:
            zero = jnp.zeros((EDGE, ref.shape[1]), ref.dtype)
            ref[:EDGE, :] = zero
            ref[ref.shape[0] - EDGE :, :] = zero


def conv_forward_kernel(place, base, p, r, gain, link, valid, taps, *refs, groups):
    blocks, (x_ref, uc, gp, dc, sums, glu) = refs[:groups], refs[groups:]
    i = pl.program_id(0)
    clear_edges(glu)
    first_step(sums)

    @pl.when(i < pl.num_programs(0) - 1)
    def _():
        a, b, c = wide(base, p, r)
        x = a + (b + c)
        x_ref[...] = x
        uc[...] = (norm_parts(x)[0] * gain[...]).astype(BF)
        n = blocks[0].shape[0]
        both = sum(dot(uc[:, columns_of(place, s, n)], w[...]) for s, w in enumerate(blocks))
        gp[...] = both.astype(BF)
        part = both.shape[1] // 2
        keep_block(glu, i, both[:, :part] * jax.nn.sigmoid(both[:, part:]))

    @pl.when(i > 0)
    def _():
        rows = window(glu, i - 1)
        out = sum(
            taken(rows, o) * (link[:, o : o + 1] * taps[o : o + 1, :]) for o in range(KER)
        )
        dc[...] = out
        counted = valid[...] * out
        sums[0:1, :] += jnp.sum(counted, axis=0, keepdims=True)
        sums[1:2, :] += jnp.sum(counted * out, axis=0, keepdims=True)
        sums[2:3, :] += jnp.sum(valid[...])


def conv_forward(place, base, p, r, gain, link, valid, taps, blocks):
    t, d = base.shape
    part = taps.shape[1]
    ins = [by_rows(base), by_rows(p), by_rows(r), all_of(gain[None])]
    ins += [by_rows(link, 1), by_rows(valid, 1), all_of(taps)] + weight_blocks(blocks, 2 * part, 0)
    outs = [out_rows((t, d), F32), out_rows((t, d), BF), out_rows((t, 2 * part), BF)]
    outs += [out_rows((t, part), F32, 1), out_all((3, part), F32)]
    kernel = functools.partial(conv_forward_kernel, groups=len(blocks))
    scratch = [pltpu.VMEM((t + 2 * EDGE, part), F32)]
    return launch(kernel, "conv_forward", t // ROWS + 1, place, ins, outs, scratch)


def batch_moments(sums):
    count = sums[2:3, :]
    mu = sums[0:1, :] / count
    return mu, lax.rsqrt(sums[1:2, :] / count - mu * mu + EPS), count


def batch_forward_kernel(place, dc, sums, gain, shift, out_w, sw, part):
    mu, rstd, _ = batch_moments(sums)
    bo = (dc[...] - mu) * rstd * gain[...] + shift[...]
    sw[...] = (bo * jax.nn.sigmoid(bo)).astype(BF)
    part[...] = dot(sw[...], out_w[...]).astype(BF)


def batch_forward(place, dc, sums, gain, shift, out_w):
    t, part = dc.shape
    d = out_w.shape[1]
    ins = [by_rows(dc), all_of(sums), all_of(gain[None]), all_of(shift[None]), all_of(out_w)]
    outs = [out_rows((t, part), BF), out_rows((t, d), BF)]
    return launch(batch_forward_kernel, "batch_forward", t // ROWS, place, ins, outs)


def back_step(g, p, r, x, gain, gg):
    gu, other = wide(p, r)
    gu = gu + other
    hat, rstd = norm_parts(x[...].astype(F32))
    gg[...] += jnp.sum(gu * hat, axis=0, keepdims=True)
    return g[...] + norm_back(gu, hat, rstd, gain[...])


def hidden_grad(pre, gf):
    a = pre[...].astype(F32)
    return dot((a * jax.nn.sigmoid(a)).astype(BF), gf[...], 0, 0).astype(BF)


def store_at(steps, refs, make):
    for j, ref in enumerate(refs):

        @pl.when(pl.program_id(0) == steps + j)
        def _(ref=ref):
            ref[...] = make()


def final_kernel(place, x, p, r, cot, gain, pre, layer, g, gf, gg, *sends):
    steps = gf.shape[0] // ROWS
    first_step(gg)
    i = pl.program_id(0)

    @pl.when(i < steps)
    def _():
        a, b, c, y = wide(x, p, r, cot)
        hat, rstd = norm_parts(a + 0.5 * (b + c))
        layer[...] = (hat * gain[...]).astype(BF)
        gg[...] += jnp.sum(y * hat, axis=0, keepdims=True)
        new = norm_back(y, hat, rstd, gain[...])
        g[...] = new
        gf[pl.ds(pl.multiple_of(i * ROWS, ROWS), ROWS), :] = (0.5 * new).astype(BF)

    store_at(steps, sends, lambda: hidden_grad(pre, gf))


def hidden_blocks(pre, steps):
    quarter = pre.shape[1] // 4
    return pre, pl.BlockSpec(
        (pre.shape[0], quarter), lambda i, place: (0, place[4 + jnp.clip(i - steps, 0, 3)])
    )


def final_down(place, x, p, r, cot, gain, pre):
    t, d = x.shape
    n = t // ROWS
    ins = [by_rows(x), by_rows(p), by_rows(r), by_rows(cot), all_of(gain[None])]
    ins += [hidden_blocks(pre, n)]
    outs = [out_rows((t, d), BF), out_rows((t, d), F32), out_all((t, d), BF), out_all((1, d), F32)]
    outs += [out_all((pre.shape[1] // 4, d), BF)] * 2
    return launch(final_kernel, "final_down", n + 2, place, ins, outs)


def keep_kernel(place, gf, pre, *keeps):
    store_at(0, keeps, lambda: hidden_grad(pre, gf))


def down_keep(place, gf, pre):
    d = gf.shape[1]
    ins = [all_of(gf), hidden_blocks(pre, -2)]
    outs = [out_all((pre.shape[1] // 4, d), BF)] * 2
    return launch(keep_kernel, "down_keep", 2, place, ins, outs)


def back_down_kernel(place, p, r, g, x, gain, pre, g_ref, gf, gg, *sends):
    steps = gf.shape[0] // ROWS
    first_step(gg)
    i = pl.program_id(0)

    @pl.when(i < steps)
    def _():
        new = back_step(g, p, r, x, gain, gg)
        g_ref[...] = new
        gf[pl.ds(pl.multiple_of(i * ROWS, ROWS), ROWS), :] = (0.5 * new).astype(BF)

    store_at(steps, sends, lambda: hidden_grad(pre, gf))


def back_down(place, p, r, g, x, gain, pre):
    t, d = x.shape
    n = t // ROWS
    ins = two_parts(p, r) + [by_rows(g), by_rows(x), all_of(gain[None]), hidden_blocks(pre, n)]
    outs = [out_rows((t, d), F32), out_all((t, d), BF), out_all((1, d), F32)]
    outs += [out_all((pre.shape[1] // 4, d), BF)] * 4
    return launch(back_down_kernel, "back_down", n + 4, place, ins, outs)


def ffn_back_kernel(place, gf, pre, up, down, part, ga):
    chunk = min(1024, up.shape[0])
    total = None
    for c in range(0, up.shape[0], chunk):
        gh = dot(gf[...], down[c : c + chunk, :], 1, 1)
        now = (gh * slope(pre[:, c : c + chunk].astype(F32))).astype(BF)
        ga[:, c : c + chunk] = now
        f = dot(now, up[c : c + chunk, :])
        total = f if total is None else total + f
    part[0] = part[1] = total.astype(BF)


def ffn_back(place, gf, pre, up, down):
    t, d = gf.shape
    hid = up.shape[0]
    ins = [by_rows(gf), by_rows(pre), all_of(up), all_of(down)]
    outs = [out_twice((t, d), BF), out_rows((t, hid), BF)]
    return launch(ffn_back_kernel, "ffn_back", t // ROWS, place, ins, outs)


def up_grad_kernel(place, ga, u, *refs):
    store_at(0, refs, lambda: dot(ga[...], u[...], 0, 0).astype(BF))


def up_grad(place, ga, u):
    d = u.shape[1]
    ins = [hidden_blocks(ga, 0), all_of(u)]
    outs = [out_all((ga.shape[1] // 4, d), BF)] * 4
    return launch(up_grad_kernel, "up_grad", 4, place, ins, outs)


def conv_back_one_kernel(
    place, p, r, g, x, gain, dc, sw, sums, bgain, bshift, out_w, g_ref, gg, gbo, ab, grad, acc
):
    first_step(gg, ab, acc)
    new = back_step(g, p, r, x, gain, gg)
    g_ref[...] = new
    low = new.astype(BF)
    mu, rstd, _ = batch_moments(sums)
    hat = (dc[...] - mu) * rstd
    back = dot(low, out_w[...], 1, 1) * slope(hat * bgain[...] + bshift[...])
    gbo[...] = back
    ab[0:1, :] += jnp.sum(back, axis=0, keepdims=True)
    ab[1:2, :] += jnp.sum(back * hat, axis=0, keepdims=True)
    acc[...] += dot(sw[...], low, 0, 0)

    @pl.when(last_step())
    def _():
        grad[...] = acc[...].astype(BF)


def conv_back_one(place, p, r, g, x, gain, dc, sw, sums, bgain, bshift, out_w):
    t, d = x.shape
    part = dc.shape[1]
    ins = two_parts(p, r) + [by_rows(g), by_rows(x), all_of(gain[None]), by_rows(dc)]
    ins += [by_rows(sw), all_of(sums), all_of(bgain[None]), all_of(bshift[None]), all_of(out_w)]
    outs = [out_rows((t, d), F32), out_all((1, d), F32), out_rows((t, part), F32)]
    outs += [out_all((2, part), F32), out_all((part, d), BF)]
    scratch = [pltpu.VMEM((part, d), F32)]
    return launch(conv_back_one_kernel, "conv_back_one", t // ROWS, place, ins, outs, scratch)


def conv_back_two_kernel(
    place, gbo, dc, gp, gp_lag, uc, link, valid, sums, ab, bgain, taps, *refs, groups
):
    blocks, (part, grad, taps_grad, gdc_s, glu_s, acc) = refs[:groups], refs[groups:]
    i = pl.program_id(0)
    width = dc.shape[1]
    clear_edges(gdc_s, glu_s)
    first_step(taps_grad, acc)

    @pl.when(i < pl.num_programs(0) - 1)
    def _():
        mu, rstd, count = batch_moments(sums)
        scaled = rstd * bgain[...]
        gvar = -0.5 * rstd * scaled * ab[1:2, :]
        mean_part = (-scaled * ab[0:1, :] - 2.0 * mu * gvar) / count
        slope_part = 2.0 * gvar / count
        gdc = gbo[...] * scaled + valid[...] * (mean_part + dc[...] * slope_part)
        keep_block(gdc_s, i, gdc)
        both = gp[...].astype(F32)
        keep_block(glu_s, i, both[:, :width] * jax.nn.sigmoid(both[:, width:]))

    @pl.when(i > 0)
    def _():
        gdc_rows, glu_rows = window(gdc_s, i - 1), window(glu_s, i - 1)
        middle = taken(gdc_rows, RIM)
        gglu = None
        for o in range(KER):
            linked = link[:, o : o + 1]
            mirror = KER - 1 - o
            term = taken(gdc_rows, o) * (linked * taps[mirror : mirror + 1, :])
            gglu = term if gglu is None else gglu + term
            taps_grad[o : o + 1, :] += jnp.sum(
                middle * (taken(glu_rows, o) * linked), axis=0, keepdims=True
            )
        both = gp_lag[...].astype(F32)
        opener = jax.nn.sigmoid(both[:, width:])
        first = gglu * opener
        second = first * both[:, :width] * (1.0 - opener)
        ggp = jnp.concatenate([first.astype(BF), second.astype(BF)], axis=1)
        n = blocks[0].shape[0]
        for s, w in enumerate(blocks):
            columns = columns_of(place, s, n)
            part[0, :, columns] = part[1, :, columns] = dot(ggp, w[...], 1, 1).astype(BF)
        acc[...] += dot(uc[...], ggp, 0, 0)

    @pl.when(last_step())
    def _():
        grad[...] = acc[...].astype(BF)


def conv_back_two(place, gbo, dc, gp, uc, link, valid, sums, ab, bgain, taps, blocks):
    t, d = uc.shape
    part = dc.shape[1]
    ins = [by_rows(gbo), by_rows(dc), by_rows(gp), by_rows(gp, 1), by_rows(uc, 1), by_rows(link, 1)]
    ins += [by_rows(valid), all_of(sums), all_of(ab), all_of(bgain[None]), all_of(taps)]
    ins += weight_blocks(blocks, 2 * part, 0)
    outs = [out_twice((t, d), BF, 1), out_all((d, 2 * part), BF), out_all((KER, part), F32)]
    scratch = [pltpu.VMEM((t + 2 * EDGE, part), F32)] * 2 + [pltpu.VMEM((d, 2 * part), F32)]
    kernel = functools.partial(conv_back_two_kernel, groups=len(blocks))
    return launch(kernel, "conv_back_two", t // ROWS + 1, place, ins, outs, scratch)


def context_back_kernel(place, p, r, g, x, gain, ctx, out_w, g_ref, gg, gctx, grad, acc):
    first_step(gg, acc)
    new = back_step(g, p, r, x, gain, gg)
    g_ref[...] = new
    low = new.astype(BF)
    gctx[...] = dot(low, out_w[...], 1, 1).astype(BF)
    acc[...] += dot(ctx[...], low, 0, 0)

    @pl.when(last_step())
    def _():
        grad[...] = acc[...].astype(BF)


def context_back(place, p, r, g, x, gain, ctx, out_w):
    t, d = x.shape
    part = ctx.shape[1]
    ins = two_parts(p, r) + [by_rows(g), by_rows(x), all_of(gain[None])]
    ins += [by_rows(ctx), all_of(out_w)]
    outs = [out_rows((t, d), F32), out_all((1, d), F32), out_rows((t, part), BF)]
    outs += [out_all((part, d), BF)]
    scratch = [pltpu.VMEM((part, d), F32)]
    return launch(context_back_kernel, "context_back", t // ROWS, place, ins, outs, scratch)


def projections_back_kernel(place, *refs, pieces, groups):
    parts, ua, refs = refs[:pieces], refs[pieces], refs[pieces + 1 :]
    blocks, (part, grad, acc) = refs[:groups], refs[groups:]
    first_step(acc)
    all3 = jnp.concatenate([p[...] for p in parts], axis=1)
    n = blocks[0].shape[0]
    for s, w in enumerate(blocks):
        columns = columns_of(place, s, n)
        part[0, :, columns] = part[1, :, columns] = dot(all3, w[...], 1, 1).astype(BF)
    acc[...] += dot(ua[...], all3, 0, 0)

    @pl.when(last_step())
    def _():
        grad[...] = acc[...].astype(BF)


def projections_back(place, *arrays):
    *parts, ua, blocks = arrays
    t, d = ua.shape
    part = sum(p.shape[1] for p in parts) // 3
    ins = [by_rows(p) for p in parts] + [by_rows(ua)] + weight_blocks(blocks, 3 * part, 1)
    outs = [out_twice((t, d), BF), out_all((d, 3 * part), BF)]
    scratch = [pltpu.VMEM((d, 3 * part), F32)]
    kernel = functools.partial(projections_back_kernel, pieces=len(parts), groups=len(blocks))
    return launch(kernel, "projections_back", t // ROWS, place, ins, outs, scratch)


def first_back_kernel(place, p, r, g, x, gain, out, gg):
    first_step(gg)
    out[...] = back_step(g, p, r, x, gain, gg).astype(BF)


def first_back(place, p, r, g, x, gain):
    t, d = x.shape
    ins = two_parts(p, r) + [by_rows(g), by_rows(x), all_of(gain[None])]
    outs = [out_rows((t, d), BF), out_all((1, d), F32)]
    return launch(first_back_kernel, "first_back", t // ROWS, place, ins, outs)


def encoding(length, features):
    half = features // 2
    frequency = jnp.exp(jnp.arange(half).astype(F32) * (-2.0 * math.log(10000.0) / features))
    fine = 32
    steps = jnp.arange(length // fine) * fine
    a = jnp.where(steps < length // 2, -steps, length - steps).astype(F32)[:, None] * frequency[None]
    b = jnp.arange(fine).astype(F32)[:, None] * frequency[None]
    sa, ca = jnp.sin(a)[:, None], jnp.cos(a)[:, None]
    sb, cb = jnp.sin(b)[None], jnp.cos(b)[None]
    sine = sa * cb - ca * sb
    cosine = ca * cb + sa * sb
    return jnp.concatenate([sine, cosine], axis=-1).reshape(length, features).astype(BF)


def on_device(
    frames,
    segment_ids,
    valid_mask,
    first_norm,
    first_up,
    first_down,
    attention_norm,
    query_proj,
    key_proj,
    value_proj,
    output_proj,
    position_proj,
    content_bias,
    position_bias,
    convolution_norm,
    pointwise_in,
    depthwise,
    batch_gain,
    batch_shift,
    pointwise_out,
    second_norm,
    second_up,
    second_down,
    final_norm,
    cotangent,
):
    groups = lax.axis_size("fsdp")
    member = lax.axis_index("fsdp")
    shard_frames, d = frames.shape[1:]
    t = segment_ids.shape[1]
    part = d // groups
    seg = segment_ids[0]
    valid = valid_mask[0].astype(F32)[:, None]
    bits = [bit_of(0), bit_of(1)]
    quarters = [1 - bits[0], 3 - bits[1], bits[0], 2 + bits[1]]
    owners = [lax.rem(member + groups - s, groups) for s in range(groups)]
    place = jnp.stack([(member + 1) % 2] + [jnp.int32(0)] * 3 + quarters + owners).astype(jnp.int32)

    def own(v, axis=0):
        return lax.dynamic_slice_in_dim(v, member * part, part, axis)

    def own_rows(v):
        return lax.dynamic_slice_in_dim(v, member * shard_frames, shard_frames, 0)[None]

    x0 = gather_rows(frames[0], place)
    seg_rim = jnp.pad(seg, (RIM, RIM), constant_values=-1)
    link = jnp.stack([(seg_rim[o : o + t] == seg).astype(F32) for o in range(KER)], axis=1)
    taps = own(depthwise).T
    gain_own, shift_own = own(batch_gain), own(batch_shift)

    if groups == 2:
        kept, away = packed(
            place,
            [(pointwise_in, 0, part), (pointwise_in, 2, part)]
            + [(m, 0, part) for m in (position_proj, query_proj, key_proj, value_proj)],
        )
        away, x0 = lax.optimization_barrier((away, x0))
        blocks = [kept, shifted(away, 1)]
    else:
        value_in, gate_in = pointwise_in[:, :d], pointwise_in[:, d:]
        blocks = own_columns(
            [(m, part) for m in (value_in, gate_in, position_proj, query_proj, key_proj, value_proj)]
        )
    part_sum, pre1, u1 = ffn_forward(place, x0, (), first_norm, first_up, first_down)
    other = pair_other(part_sum)
    encoded = encoding(t, d)
    pos = sum(
        dot(
            lax.dynamic_slice_in_dim(encoded, owner * part, part, 1),
            block[:, 2 * part : 3 * part],
        )
        for owner, block in zip(owners, blocks, strict=True)
    ).astype(BF)
    x1, ua, qc, qp, keys, values = qkv_forward(
        place, x0, part_sum, other, attention_norm, own(content_bias), own(position_bias), blocks
    )
    cotangent, _ = lax.optimization_barrier((cotangent, x1))
    cot = gather_rows(cotangent[0], place)
    ctx, part_sum = attention(place, seg, qc, qp, keys, values, pos, output_proj)
    other = pair_other(part_sum)
    x2, uc, gp, dc, sums = conv_forward(
        place, x1, part_sum, other, convolution_norm, link, valid, taps, blocks
    )
    sums = row_sum(sums)
    sw, part_sum = batch_forward(place, dc, sums, gain_own, shift_own, pointwise_out)
    other = pair_other(part_sum)
    x3, part_sum, pre2, u2 = ffn_forward(
        place, x2, (part_sum, other), second_norm, second_up, second_down
    )
    other = pair_other(part_sum)

    sequence = Sequence()
    run = sequence.run
    sums_of = {}
    plan = list(PLAN)

    def ready(name, arrays, parts=None):
        sums_of[name] = BatchSum(sequence, arrays, parts)
        if parts is not None:
            sums_of[name].step()

    def comm():
        for name in plan.pop(0):
            sums_of[name].step()

    hid = second_up.shape[0]
    layer_out, g, gf, final_gain, send0, send1 = final_down(
        place, x3, part_sum, other, cot, final_norm, pre2
    )
    keep = run(lambda *v: down_keep(place, *v), gf, pre2)
    ready("a", [hid], (tuple(keep), (send0, send1)))
    comm()
    part_sum, ga = run(lambda *v: ffn_back(place, *v), gf, pre2, second_up, second_down)
    comm()
    (part_sum,) = sequence.tie(part_sum)
    other = pair_swap(part_sum)
    quads = run(lambda *v: up_grad(place, *v), ga, u2)
    comm()
    g, second_gain, gbo, ab, out_w_grad = run(
        lambda *v: conv_back_one(place, *v),
        part_sum, other, g, x3, second_norm, dc, sw, sums, gain_own, shift_own, pointwise_out,
    )
    comm()
    (ab,) = sequence.tie(ab)
    ab = row_sum(ab)
    sequence.last = ab
    comm()
    quads = sequence.tie(*quads)
    ready("b", [hid], ((quads[2], quads[3]), (quads[0], quads[1])))
    part_sum, in_w_grad, taps_grad = run(
        lambda ab, gbo: conv_back_two(
            place, gbo, dc, gp, uc, link, valid, sums, ab, gain_own, taps, blocks
        ),
        ab,
        gbo,
    )
    comm()
    part_sum, in_w_grad = sequence.tie(part_sum, in_w_grad)
    other = pair_swap(part_sum)
    swapped = row_blocks_swap(in_w_grad)

    def unfold(swapped, at):
        columns = slice(at * part, (at + 1) * part)
        return jnp.concatenate([swapped[j][:, columns] for j in range(groups)], axis=1)

    ready("c", [out_w_grad, unfold(swapped, 0), unfold(swapped, 1)])
    comm()
    g, conv_gain, gctx, output_grad = run(
        lambda *v: context_back(place, *v),
        part_sum, other, g, x2, convolution_norm, ctx, output_proj,
    )
    comm()
    halves_of = []
    for first in (True, False):
        half = run(
            lambda *v, first=first: attention_back(place, seg, *v, first),
            qc, qp, keys, values, pos, gctx,
        )
        if half is not None:
            halves_of.append(half)
        comm()
    gqkv = [h[at] for at in range(3) for h in halves_of]
    gpos, content_grad, position_grad = (
        jnp.concatenate([h[at] for h in halves_of], axis=1) for at in range(3, 6)
    )
    part_sum, qkv_grad = run(lambda *v: projections_back(place, *v, blocks), *gqkv, ua)
    comm()
    part_sum, qkv_grad = sequence.tie(part_sum, qkv_grad)
    other = pair_swap(part_sum)
    high = gpos.astype(BF)
    low = (gpos - high.astype(F32)).astype(BF)
    pos_grad = (dot(encoded, high, 0, 0) + dot(encoded, low, 0, 0)).astype(BF)
    swapped = row_blocks_swap(jnp.concatenate([qkv_grad, pos_grad], axis=1))
    ready("d", [output_grad] + [unfold(swapped, at) for at in range(4)])
    comm()
    g, gf, attention_gain, *quads = run(
        lambda *v: back_down(place, *v), part_sum, other, g, x1, attention_norm, pre1
    )
    ready("e", [hid], ((quads[2], quads[3]), (quads[0], quads[1])))
    comm()
    part_sum, ga = run(lambda *v: ffn_back(place, *v), gf, pre1, first_up, first_down)
    comm()
    (part_sum,) = sequence.tie(part_sum)
    other = pair_swap(part_sum)
    quads = run(lambda *v: up_grad(place, *v), ga, u1)
    ready("f", [hid], ((quads[2], quads[3]), (quads[0], quads[1])))
    comm()
    frames_grad, first_gain = run(
        lambda *v: first_back(place, *v), part_sum, other, g, x0, first_norm
    )
    gains = [own(v[0]) for v in (first_gain, attention_gain, conv_gain, second_gain, final_gain)]
    small = jnp.concatenate(
        [jnp.stack(gains), content_grad, position_grad, taps_grad], axis=0
    )
    sums_of["s"] = SmallSum(sequence, small)
    comm()
    for job in sums_of.values():
        job.finish()
    small = sums_of["s"].v
    out_w_grad, value_grad, gate_grad = sums_of["c"].out
    output_grad, q_grad, k_grad, v_grad, pos_grad = sums_of["d"].out
    return (
        own_rows(layer_out),
        own_rows(frames_grad),
        small[0],
        sums_of["f"].out[0],
        sums_of["e"].out[0],
        small[1],
        q_grad,
        k_grad,
        v_grad,
        output_grad,
        pos_grad,
        small[5],
        small[6],
        small[2],
        jnp.concatenate([value_grad, gate_grad], axis=1),
        small[7:].T,
        ab[1],
        ab[0],
        out_w_grad,
        small[3],
        sums_of["b"].out[0],
        sums_of["a"].out[0],
        small[4],
    )


def solution(mesh):
    rows, shard, whole = P("batch", "fsdp", None), P("fsdp", None), P()
    return jax.shard_map(
        on_device,
        mesh=mesh,
        in_specs=(
            rows,
            P("batch", None),
            P("batch", None),
            whole,
            shard,
            shard,
            whole,
            shard,
            shard,
            shard,
            shard,
            shard,
            whole,
            whole,
            whole,
            shard,
            whole,
            whole,
            whole,
            shard,
            whole,
            shard,
            shard,
            whole,
            rows,
        ),
        out_specs=(
            rows,
            rows,
            P("fsdp"),
            shard,
            shard,
            P("fsdp"),
            shard,
            shard,
            shard,
            shard,
            shard,
            P("fsdp"),
            P("fsdp"),
            P("fsdp"),
            shard,
            shard,
            P("fsdp"),
            P("fsdp"),
            shard,
            P("fsdp"),
            shard,
            shard,
            P("fsdp"),
        ),
        check_vma=False,
    )
```

```python
import functools
import math

import jax
import jax.numpy as jnp
from jax import lax
from jax.experimental import pallas as pl
from jax.experimental.pallas import tpu as pltpu
from jax.sharding import PartitionSpec as P

H = 8
DH = 128
KER = 5
RIM = (KER - 1) // 2
EPS = 1e-05
NEG = -1e30
BF = jnp.bfloat16
F32 = jnp.float32
VMEM = 56 * 1024 * 1024
PLAN = ("", "a", "", "a", "a", "", "ba", "a", "bcab", "c", "b", "cdbac", "dc", "e", "bdceedb", "feescfdscfesdfesfdfsdf")


def dot(a, b, da=1, db=0):
    return lax.dot_general(a, b, (((da,), (db,)), ((), ())), preferred_element_type=F32)


def norm_parts(v):
    centred = v - jnp.mean(v, axis=-1, keepdims=True)
    rstd = lax.rsqrt(jnp.mean(centred * centred, axis=-1, keepdims=True) + EPS)
    return centred * rstd, rstd


def norm_back(grad, hat, rstd, gain):
    scaled = grad * gain
    first = jnp.mean(scaled, axis=-1, keepdims=True)
    second = jnp.mean(scaled * hat, axis=-1, keepdims=True)
    return rstd * (scaled - first - hat * second)


def slope(v):
    s = jax.nn.sigmoid(v)
    return s * (1.0 + v * (1.0 - s))


def shifted(v, s):
    g = lax.axis_size("fsdp")
    return lax.ppermute(v, "fsdp", [(i, (i + s) % g) for i in range(g)])


def natural(blocks):
    g = len(blocks)
    me = lax.axis_index("fsdp")
    if g == 1:
        return blocks[0][None]
    if g == 2:
        a, b = blocks
        return jnp.where(me == 0, jnp.stack([a, b]), jnp.stack([b, a]))
    stacked = jnp.stack(blocks[::-1])
    return jnp.roll(stacked, me + 1, axis=0)


def gather_rows(v, place):
    g = lax.axis_size("fsdp")
    if g == 2:
        return placed(place, v, shifted(v, 1))
    out = natural([v] + [shifted(v, s) for s in range(1, g)])
    return out.reshape((g * v.shape[0],) + v.shape[1:])


def pair_swap(v):
    g = lax.axis_size("fsdp")
    if g == 2:
        return lax.all_to_all(v, "fsdp", 0, 0)
    other = pair_other(v[0])
    return jnp.stack([other, other])


def pair_other(v):
    g = lax.axis_size("fsdp")
    if g == 2:
        return shifted(v, 1)
    return sum(shifted(v, s).astype(F32) for s in range(1, g))


def row_blocks_swap(v):
    g = lax.axis_size("fsdp")
    n = v.shape[0] // g
    return lax.all_to_all(v.reshape(g, n, v.shape[1]), "fsdp", 0, 0)


def own_columns(matrices):
    g = lax.axis_size("fsdp")
    me = lax.axis_index("fsdp")

    def columns(member):
        parts = []
        for m, width in matrices:
            parts.append(lax.dynamic_slice_in_dim(m, member * width, width, 1))
        return jnp.concatenate(parts, axis=1)

    blocks = [columns(me)]
    for s in range(1, g):
        blocks.append(shifted(columns(lax.rem(me + s, g)), s))
    return blocks


def bit_of(b):
    return (lax.axis_index("batch") >> b) & 1


def exchange(v, b):
    n = lax.axis_size("batch")
    return lax.ppermute(v, "batch", [(i, i ^ (1 << b)) for i in range(n)])


def is_power(n):
    return n & (n - 1) == 0


def row_sum(v):
    n = lax.axis_size("batch")
    if not is_power(n):
        return lax.psum(v, "batch")
    for b in range(n.bit_length() - 1):
        v = v + exchange(v, b)
    return v


def add16(a, b):
    return (a.astype(F32) + b.astype(F32)).astype(BF)


def halves(v, b):
    half = v.shape[0] // 2
    mine = bit_of(b)
    keep = lax.dynamic_slice_in_dim(v, mine * half, half, 0)
    return keep, lax.dynamic_slice_in_dim(v, (1 - mine) * half, half, 0)


def joined(v, other, b):
    low, high = jnp.concatenate([v, other], 0), jnp.concatenate([other, v], 0)
    return jnp.where(bit_of(b) == 1, high, low)


class Sequence:
    def __init__(self):
        self.last = None

    def run(self, step, *inputs):
        if self.last is not None:
            *inputs, _ = lax.optimization_barrier((*inputs, self.last))
        outputs = step(*inputs)
        leaves = jax.tree.leaves(outputs)
        self.last = leaves[0] if leaves else self.last
        return outputs


    def tie(self, *values):
        if self.last is None:
            return values
        return lax.optimization_barrier((*values, self.last))[:-1]


class BatchSum:
    def __init__(self, sequence, arrays, parts=None):
        self.sequence = sequence
        self.parts = parts
        self.sizes = arrays if parts is not None else [a.shape[0] for a in arrays]
        self.arrays = arrays
        bits = lax.axis_size("batch").bit_length() - 1
        rest = list(range(3, bits))
        self.bits = list(zip([0, 2, 1] + rest, [1, 2, 0] + rest, strict=True))
        self.event = 0
        self.out = None

    def send(self, k, pair):
        a, b = self.bits[k]
        if a == b:
            got = exchange(pair, a)
            return got[0], got[1]
        return exchange(pair[0], a), exchange(pair[1], b)

    def launch(self, k, now):
        a, b = self.bits[k]
        parts = [halves(now[0], a), halves(now[1], b)]
        keep, away = tuple(p[0] for p in parts), tuple(p[1] for p in parts)
        return keep, (jnp.stack(away) if a == b else away)

    def step(self):
        e, n = self.event, len(self.bits)
        self.event += 1
        if e == 0 and self.parts is not None:
            self.keep, away = self.parts
            self.got = self.send(0, away)
        elif e == 0:

            def first(*arrays):
                whole = jnp.concatenate(arrays, 0) if len(arrays) > 1 else arrays[0]
                half = whole.shape[0] // 2
                return self.launch(0, (whole[:half], whole[half:]))

            self.keep, away = self.sequence.run(first, *self.arrays)
            self.got = self.send(0, away)
        elif e < n:

            def add(k0, k1, g0, g1):
                now = (add16(k0, g0), add16(k1, g1))
                if e < n - 1:
                    return self.launch(e, now)
                return (jnp.stack(now),)

            out = self.sequence.run(add, *self.keep, *self.got)
            if e < n - 1:
                self.keep, away = out
                self.got = self.send(e, away)
            else:
                self.keep = out[0]
                self.got = exchange(self.keep, self.bits[e][0])
        elif e == n:

            def last(k, g):
                now = add16(k, g)
                return self.spread(n - 2, (now[0], now[1]))

            now = self.sequence.run(last, self.keep, self.got)
            self.forward(n - 2, now)
        elif e < 2 * n - 1:
            k = 2 * n - 2 - e

            def more(c0, c1, g0, g1):
                a, b = self.bits[k + 1]
                return self.spread(k, (joined(c0, g0, a), joined(c1, g1, b)))

            now = self.sequence.run(more, *self.now, *self.got)
            self.forward(k, now)
        else:

            def final(c0, c1, g0, g1):
                a, b = self.bits[0]
                whole = jnp.concatenate([joined(c0, g0, a), joined(c1, g1, b)], 0)
                out, at = [], 0
                for size in self.sizes:
                    out.append(whole[at : at + size].astype(F32))
                    at += size
                return out

            self.out = self.sequence.run(final, *self.now, *self.got)

    def spread(self, k, now):
        a, b = self.bits[k]
        return jnp.stack(now) if a == b else now

    def forward(self, k, now):
        self.now = (now[0], now[1])
        self.got = self.send(k, now)

    def finish(self):
        while self.out is None:
            self.step()
        return self.out


class SmallSum:
    def __init__(self, sequence, v):
        self.sequence = sequence
        self.v = v
        self.bit = 0
        self.got = exchange(v, 0)
        self.bits = lax.axis_size("batch").bit_length() - 1

    def step(self):
        if self.bit == self.bits:
            return
        self.v = self.sequence.run(lambda a, b: a + b, self.v, self.got)
        self.bit += 1
        if self.bit < self.bits:
            self.got = exchange(self.v, self.bit)

    def finish(self):
        while self.bit < self.bits:
            self.step()
        return self.v


ROWS = 256
CHEAP = pl.CostEstimate(flops=1, bytes_accessed=1, transcendentals=0)


def launch(kernel, name, steps, place, ins, outs, scratch=()):
    return pl.pallas_call(
        kernel,
        grid_spec=pltpu.PrefetchScalarGridSpec(
            num_scalar_prefetch=1,
            grid=(steps,),
            in_specs=[spec for _, spec in ins],
            out_specs=[spec for _, _, spec in outs],
            scratch_shapes=list(scratch),
        ),
        out_shape=[jax.ShapeDtypeStruct(shape, kind) for shape, kind, _ in outs],
        compiler_params=pltpu.CompilerParams(vmem_limit_bytes=VMEM),
        cost_estimate=CHEAP,
        name=name,
    )(place, *[a for a, _ in ins])


def whole(shape):
    return pl.BlockSpec(tuple(shape), lambda i, place: (0,) * len(shape))


def all_of(a):
    return a, whole(a.shape)


def blocks_of(shape, lag=0):
    last = shape[0] // ROWS - 1
    return pl.BlockSpec((ROWS, shape[1]), lambda i, place: (jnp.clip(i - lag, 0, last), 0))


def by_rows(a, lag=0):
    return a, blocks_of(a.shape, lag)


def out_rows(shape, kind, lag=0):
    return shape, kind, blocks_of(shape, lag)


def out_twice(shape, kind, lag=0):
    last = shape[0] // ROWS - 1
    spec = pl.BlockSpec((2, ROWS, shape[1]), lambda i, place: (0, jnp.clip(i - lag, 0, last), 0))
    return (2, *shape), kind, spec


def two_parts(part, other):
    last = part.shape[1] // ROWS - 1
    block = (None, ROWS, part.shape[2])
    return [
        (part, pl.BlockSpec(block, lambda i, place: (0, jnp.minimum(i, last), 0))),
        (other, pl.BlockSpec(block, lambda i, place: (place[0], jnp.minimum(i, last), 0))),
    ]


def out_all(shape, kind):
    return shape, kind, whole(shape)


def columns_of(place, s, width):
    return pl.ds(pl.multiple_of(place[8 + s] * width, width), width)


def first_step(*refs):
    @pl.when(pl.program_id(0) == 0)
    def _():
        for ref in refs:
            ref[...] = jnp.zeros_like(ref)


def last_step():
    return pl.program_id(0) == pl.num_programs(0) - 1


def wide(*refs):
    return [ref[...].astype(F32) for ref in refs]


def placed_kernel(place, own, other, out):
    @pl.when(pl.program_id(0) == 0)
    def _():
        out[...] = own[...]

    @pl.when(pl.program_id(0) == 1)
    def _():
        out[...] = other[...]


def placed(place, own, other):
    n, d = own.shape
    spec = pl.BlockSpec((n, d), lambda i, place: ((place[0] + 1 + i) % 2, 0))
    ins, outs = [all_of(own), all_of(other)], [((2 * n, d), own.dtype, spec)]
    return launch(placed_kernel, "placed", 2, place, ins, outs)[0]


def pack_kernel(place, *refs):
    half = len(refs) // 2 - 1
    own, away = refs[-2:]
    width = refs[0].shape[1]
    for j in range(half):
        columns = slice(j * width, (j + 1) * width)
        own[:, columns] = refs[j][...]
        away[:, columns] = refs[half + j][...]


def packed(place, matrices):
    n = matrices[0][0].shape[0]
    width = matrices[0][2]

    def part(m, first, mine):
        def at(i, place):
            member = (place[0] + 1) % 2 if mine else place[0]
            return (0, first + member)

        return m, pl.BlockSpec((n, width), at)

    ins = [part(m, first, mine) for mine in (True, False) for m, first, _ in matrices]
    outs = [((n, len(matrices) * width), BF, whole((n, len(matrices) * width)))] * 2
    return launch(pack_kernel, "packed", 1, place, ins, outs)


def ffn_forward_kernel(place, *refs, joined):
    if joined:
        base, p, r, gain, up, down, x_ref, part, pre, u_ref = refs
        a, b, c = wide(base, p, r)
        x = a + (b + c)
        x_ref[...] = x
    else:
        base, gain, up, down, part, pre, u_ref = refs
        (x,) = wide(base)
    u = (norm_parts(x)[0] * gain[...]).astype(BF)
    u_ref[...] = u
    chunk = min(1024, up.shape[0])
    total = None
    for c in range(0, up.shape[0], chunk):
        a = dot(u, up[c : c + chunk, :], 1, 1)
        pre[:, c : c + chunk] = a.astype(BF)
        h = (a * jax.nn.sigmoid(a)).astype(BF)
        f = dot(h, down[c : c + chunk, :])
        total = f if total is None else total + f
    part[...] = total.astype(BF)


def ffn_forward(place, base, pair, gain, up, down):
    t, d = base.shape
    hid = up.shape[0]
    ins = [by_rows(base)] + [by_rows(v) for v in pair] + [all_of(gain[None]), all_of(up), all_of(down)]
    outs = [out_rows((t, d), BF), out_rows((t, hid), BF), out_rows((t, d), BF)]
    if pair:
        outs = [out_rows((t, d), F32)] + outs
    kernel = functools.partial(ffn_forward_kernel, joined=bool(pair))
    return launch(kernel, "ffn_forward", t // ROWS, place, ins, outs)


def qkv_kernel(place, base, p, r, gain, content, position, *refs, groups):
    blocks, (x_ref, ua, qc, qp, k, v) = refs[:groups], refs[groups:]
    a, b, c = wide(base, p, r)
    x = a + 0.5 * (b + c)
    x_ref[...] = x
    ua[...] = (norm_parts(x)[0] * gain[...]).astype(BF)
    n = blocks[0].shape[0]
    all3 = sum(dot(ua[:, columns_of(place, s, n)], w[...]) for s, w in enumerate(blocks))
    part = qc.shape[1]
    q = all3[:, :part]
    qc[...] = (q + content[...]).astype(BF)
    qp[...] = (q + position[...]).astype(BF)
    k[...] = all3[:, part : 2 * part].astype(BF)
    v[...] = all3[:, 2 * part :].astype(BF)


def weight_blocks(blocks, width, at):
    return [(w, pl.BlockSpec((w.shape[0], width), lambda i, place: (0, at))) for w in blocks]


def qkv_forward(place, base, p, r, gain, content, position, blocks):
    t, d = base.shape
    part = content.shape[0]
    ins = [by_rows(base), by_rows(p), by_rows(r)]
    ins += [all_of(v[None]) for v in (gain, content, position)] + weight_blocks(blocks, 3 * part, 1)
    outs = [out_rows((t, d), F32), out_rows((t, d), BF)] + [out_rows((t, part), BF)] * 4
    kernel = functools.partial(qkv_kernel, groups=len(blocks))
    return launch(kernel, "qkv", t // ROWS, place, ins, outs)


def turned(rows, length):
    return pl.ds(pl.multiple_of(lax.rem(length - pl.program_id(0) * rows, length), rows), length)


def fill_twice(twice_ref, pos_ref):
    length = pos_ref.shape[0]

    @pl.when(pl.program_id(0) == 0)
    def _():
        twice_ref[:length, :] = pos_ref[...]
        twice_ref[length:, :] = pos_ref[...]


def exponentials(same, qc, qp, k, pos):
    far = pltpu.roll(dot(qp, pos, 1, 1), 0, 1, stride=1, stride_axis=0)
    z = jnp.where(same, dot(qc, k, 1, 1) + far, NEG)
    e = jnp.exp2((z - jnp.max(z, axis=1, keepdims=True)) * (math.log2(math.e) / math.sqrt(DH)))
    return e, 1.0 / jnp.sum(e, axis=1, keepdims=True)


def attention_kernel(place, segq, segk, qc, qp, k, v, pos, out_w, ctx, part, twice):
    fill_twice(twice, pos)
    at = turned(qc.shape[0], k.shape[0])
    same = segq[...] == segk[...]
    for h in range(qc.shape[1] // DH):
        c = slice(h * DH, (h + 1) * DH)
        e, inverse = exponentials(same, qc[:, c], qp[:, c], k[:, c], twice[at, c])
        ctx[:, c] = (dot(e.astype(BF), v[:, c]) * inverse).astype(BF)
    part[...] = dot(ctx[...], out_w[...]).astype(BF)


def attention(place, seg, qc, qp, k, v, pos, out_w):
    t, width = qc.shape
    d = out_w.shape[1]
    ins = [by_rows(seg[:, None]), all_of(seg[None]), by_rows(qc), by_rows(qp)]
    ins += [all_of(a) for a in (k, v, pos, out_w)]
    outs = [out_rows((t, width), BF), out_rows((t, d), BF)]
    scratch = [pltpu.VMEM((2 * t, width), BF)]
    return launch(attention_kernel, "attention_forward", t // ROWS, place, ins, outs, scratch)


def attention_back_kernel(
    place, segq, segk, qc, qp, k, v, pos, gctx,
    gq, gk, gv, gpos, content, position, gk_acc, gv_acc, twice, gpos_acc,
):
    rows, length = qc.shape[0], k.shape[0]
    first_step(gk_acc, gv_acc, gpos_acc, content, position)
    fill_twice(twice, pos)
    at = turned(rows, length)
    same = segq[...] == segk[...]
    at_row = lax.broadcasted_iota(jnp.int32, (rows, rows), 0)
    at_col = lax.broadcasted_iota(jnp.int32, (rows, rows), 1)
    flip = jnp.where(at_row + at_col == rows - 1, 1.0, 0.0).astype(BF)
    for h in range(qc.shape[1] // DH):
        c = slice(h * DH, (h + 1) * DH)
        near = twice[at, c]
        e, inverse = exponentials(same, qc[:, c], qp[:, c], k[:, c], near)
        prob = e * inverse
        gout = gctx[:, c]
        gprob = dot(gout, v[:, c], 1, 1)
        gv_acc[:, c] += dot(prob.astype(BF), gout, 0, 0)
        inner = jnp.sum(prob * gprob, axis=1, keepdims=True)
        gz = (prob * (gprob - inner) * (1.0 / math.sqrt(DH))).astype(BF)
        gqc = dot(gz, k[:, c])
        gk_acc[:, c] += dot(gz, qc[:, c], 0, 0)
        skew = pltpu.roll(dot(flip, gz), length - rows + 1, 1, stride=1, stride_axis=0).astype(BF)
        gqp = dot(skew, near)
        gpos_acc[at, c] += dot(skew, dot(flip, qp[:, c]).astype(BF), 0, 0)
        gq[:, c] = (gqc + dot(flip, gqp.astype(BF))).astype(BF)
        content[:, c] += jnp.sum(gqc, axis=0, keepdims=True)
        position[:, c] += jnp.sum(gqp, axis=0, keepdims=True)

    @pl.when(last_step())
    def _():
        gk[...] = gk_acc[...].astype(BF)
        gv[...] = gv_acc[...].astype(BF)
        gpos[...] = gpos_acc[:length, :] + gpos_acc[length:, :]


def attention_back(place, seg, qc, qp, k, v, pos, gctx, first):
    t, width = qc.shape
    if (width // DH) % 2 == 0:
        width //= 2
    elif not first:
        return None
    at = 0 if first else 1

    def columns(a, rows):
        return a, pl.BlockSpec((rows, width), lambda i, place: (i if rows < t else 0, at))

    ins = [by_rows(seg[:, None]), all_of(seg[None]), columns(qc, ROWS), columns(qp, ROWS)]
    ins += [columns(a, t) for a in (k, v, pos)] + [columns(gctx, ROWS)]
    outs = [out_rows((t, width), BF), out_all((t, width), BF), out_all((t, width), BF)]
    outs += [out_all((t, width), F32), out_all((1, width), F32), out_all((1, width), F32)]
    scratch = [pltpu.VMEM((t, width), F32)] * 2
    scratch += [pltpu.VMEM((2 * t, width), BF), pltpu.VMEM((2 * t, width), F32)]
    return launch(attention_back_kernel, "attention_back", t // ROWS, place, ins, outs, scratch)


EDGE = 8


def window(ref, block):
    return ref[pl.ds(pl.multiple_of(block * ROWS, ROWS), ROWS + 2 * EDGE), :]


def taken(rows, o):
    return rows[EDGE - RIM + o : EDGE - RIM + o + ROWS, :]


def keep_block(ref, block, rows):
    ref[pl.ds(pl.multiple_of(block * ROWS + EDGE, EDGE), ROWS), :] = rows


def clear_edges(*refs):
    @pl.when(pl.program_id(0) == 0)
    def _():
        for ref in refs:
            zero = jnp.zeros((EDGE, ref.shape[1]), ref.dtype)
            ref[:EDGE, :] = zero
            ref[ref.shape[0] - EDGE :, :] = zero


def conv_forward_kernel(place, base, p, r, gain, link, valid, taps, *refs, groups):
    blocks, (x_ref, uc, gp, dc, sums, glu) = refs[:groups], refs[groups:]
    i = pl.program_id(0)
    clear_edges(glu)
    first_step(sums)

    @pl.when(i < pl.num_programs(0) - 1)
    def _():
        a, b, c = wide(base, p, r)
        x = a + (b + c)
        x_ref[...] = x
        uc[...] = (norm_parts(x)[0] * gain[...]).astype(BF)
        n = blocks[0].shape[0]
        both = sum(dot(uc[:, columns_of(place, s, n)], w[...]) for s, w in enumerate(blocks))
        gp[...] = both.astype(BF)
        part = both.shape[1] // 2
        keep_block(glu, i, both[:, :part] * jax.nn.sigmoid(both[:, part:]))

    @pl.when(i > 0)
    def _():
        rows = window(glu, i - 1)
        out = sum(
            taken(rows, o) * (link[:, o : o + 1] * taps[o : o + 1, :]) for o in range(KER)
        )
        dc[...] = out
        counted = valid[...] * out
        sums[0:1, :] += jnp.sum(counted, axis=0, keepdims=True)
        sums[1:2, :] += jnp.sum(counted * out, axis=0, keepdims=True)
        sums[2:3, :] += jnp.sum(valid[...])


def conv_forward(place, base, p, r, gain, link, valid, taps, blocks):
    t, d = base.shape
    part = taps.shape[1]
    ins = [by_rows(base), by_rows(p), by_rows(r), all_of(gain[None])]
    ins += [by_rows(link, 1), by_rows(valid, 1), all_of(taps)] + weight_blocks(blocks, 2 * part, 0)
    outs = [out_rows((t, d), F32), out_rows((t, d), BF), out_rows((t, 2 * part), BF)]
    outs += [out_rows((t, part), F32, 1), out_all((3, part), F32)]
    kernel = functools.partial(conv_forward_kernel, groups=len(blocks))
    scratch = [pltpu.VMEM((t + 2 * EDGE, part), F32)]
    return launch(kernel, "conv_forward", t // ROWS + 1, place, ins, outs, scratch)


def batch_moments(sums):
    count = sums[2:3, :]
    mu = sums[0:1, :] / count
    return mu, lax.rsqrt(sums[1:2, :] / count - mu * mu + EPS), count


def batch_forward_kernel(place, dc, sums, gain, shift, out_w, sw, part):
    mu, rstd, _ = batch_moments(sums)
    bo = (dc[...] - mu) * rstd * gain[...] + shift[...]
    sw[...] = (bo * jax.nn.sigmoid(bo)).astype(BF)
    part[...] = dot(sw[...], out_w[...]).astype(BF)


def batch_forward(place, dc, sums, gain, shift, out_w):
    t, part = dc.shape
    d = out_w.shape[1]
    ins = [by_rows(dc), all_of(sums), all_of(gain[None]), all_of(shift[None]), all_of(out_w)]
    outs = [out_rows((t, part), BF), out_rows((t, d), BF)]
    return launch(batch_forward_kernel, "batch_forward", t // ROWS, place, ins, outs)


def back_step(g, p, r, x, gain, gg):
    gu, other = wide(p, r)
    gu = gu + other
    hat, rstd = norm_parts(x[...].astype(F32))
    gg[...] += jnp.sum(gu * hat, axis=0, keepdims=True)
    return g[...] + norm_back(gu, hat, rstd, gain[...])


def hidden_grad(pre, gf):
    a = pre[...].astype(F32)
    return dot((a * jax.nn.sigmoid(a)).astype(BF), gf[...], 0, 0).astype(BF)


def store_at(steps, refs, make):
    for j, ref in enumerate(refs):

        @pl.when(pl.program_id(0) == steps + j)
        def _(ref=ref):
            ref[...] = make()


def final_kernel(place, x, p, r, cot, gain, pre, layer, g, gf, gg, *sends):
    steps = gf.shape[0] // ROWS
    first_step(gg)
    i = pl.program_id(0)

    @pl.when(i < steps)
    def _():
        a, b, c, y = wide(x, p, r, cot)
        hat, rstd = norm_parts(a + 0.5 * (b + c))
        layer[...] = (hat * gain[...]).astype(BF)
        gg[...] += jnp.sum(y * hat, axis=0, keepdims=True)
        new = norm_back(y, hat, rstd, gain[...])
        g[...] = new
        gf[pl.ds(pl.multiple_of(i * ROWS, ROWS), ROWS), :] = (0.5 * new).astype(BF)

    store_at(steps, sends, lambda: hidden_grad(pre, gf))


def hidden_blocks(pre, steps):
    quarter = pre.shape[1] // 4
    return pre, pl.BlockSpec(
        (pre.shape[0], quarter), lambda i, place: (0, place[4 + jnp.clip(i - steps, 0, 3)])
    )


def final_down(place, x, p, r, cot, gain, pre):
    t, d = x.shape
    n = t // ROWS
    ins = [by_rows(x), by_rows(p), by_rows(r), by_rows(cot), all_of(gain[None])]
    ins += [hidden_blocks(pre, n)]
    outs = [out_rows((t, d), BF), out_rows((t, d), F32), out_all((t, d), BF), out_all((1, d), F32)]
    outs += [out_all((pre.shape[1] // 4, d), BF)] * 2
    return launch(final_kernel, "final_down", n + 2, place, ins, outs)


def keep_kernel(place, gf, pre, *keeps):
    store_at(0, keeps, lambda: hidden_grad(pre, gf))


def down_keep(place, gf, pre):
    d = gf.shape[1]
    ins = [all_of(gf), hidden_blocks(pre, -2)]
    outs = [out_all((pre.shape[1] // 4, d), BF)] * 2
    return launch(keep_kernel, "down_keep", 2, place, ins, outs)


def back_down_kernel(place, p, r, g, x, gain, pre, g_ref, gf, gg, *sends):
    steps = gf.shape[0] // ROWS
    first_step(gg)
    i = pl.program_id(0)

    @pl.when(i < steps)
    def _():
        new = back_step(g, p, r, x, gain, gg)
        g_ref[...] = new
        gf[pl.ds(pl.multiple_of(i * ROWS, ROWS), ROWS), :] = (0.5 * new).astype(BF)

    store_at(steps, sends, lambda: hidden_grad(pre, gf))


def back_down(place, p, r, g, x, gain, pre):
    t, d = x.shape
    n = t // ROWS
    ins = two_parts(p, r) + [by_rows(g), by_rows(x), all_of(gain[None]), hidden_blocks(pre, n)]
    outs = [out_rows((t, d), F32), out_all((t, d), BF), out_all((1, d), F32)]
    outs += [out_all((pre.shape[1] // 4, d), BF)] * 4
    return launch(back_down_kernel, "back_down", n + 4, place, ins, outs)


def ffn_back_kernel(place, gf, pre, up, down, part, ga):
    chunk = min(1024, up.shape[0])
    total = None
    for c in range(0, up.shape[0], chunk):
        gh = dot(gf[...], down[c : c + chunk, :], 1, 1)
        now = (gh * slope(pre[:, c : c + chunk].astype(F32))).astype(BF)
        ga[:, c : c + chunk] = now
        f = dot(now, up[c : c + chunk, :])
        total = f if total is None else total + f
    part[0] = part[1] = total.astype(BF)


def ffn_back(place, gf, pre, up, down):
    t, d = gf.shape
    hid = up.shape[0]
    ins = [by_rows(gf), by_rows(pre), all_of(up), all_of(down)]
    outs = [out_twice((t, d), BF), out_rows((t, hid), BF)]
    return launch(ffn_back_kernel, "ffn_back", t // ROWS, place, ins, outs)


def up_grad_kernel(place, ga, u, *refs):
    store_at(0, refs, lambda: dot(ga[...], u[...], 0, 0).astype(BF))


def up_grad(place, ga, u):
    d = u.shape[1]
    ins = [hidden_blocks(ga, 0), all_of(u)]
    outs = [out_all((ga.shape[1] // 4, d), BF)] * 4
    return launch(up_grad_kernel, "up_grad", 4, place, ins, outs)


def conv_back_one_kernel(
    place, p, r, g, x, gain, dc, sw, sums, bgain, bshift, out_w, g_ref, gg, gbo, ab, grad, acc
):
    first_step(gg, ab, acc)
    new = back_step(g, p, r, x, gain, gg)
    g_ref[...] = new
    low = new.astype(BF)
    mu, rstd, _ = batch_moments(sums)
    hat = (dc[...] - mu) * rstd
    back = dot(low, out_w[...], 1, 1) * slope(hat * bgain[...] + bshift[...])
    gbo[...] = back
    ab[0:1, :] += jnp.sum(back, axis=0, keepdims=True)
    ab[1:2, :] += jnp.sum(back * hat, axis=0, keepdims=True)
    acc[...] += dot(sw[...], low, 0, 0)

    @pl.when(last_step())
    def _():
        grad[...] = acc[...].astype(BF)


def conv_back_one(place, p, r, g, x, gain, dc, sw, sums, bgain, bshift, out_w):
    t, d = x.shape
    part = dc.shape[1]
    ins = two_parts(p, r) + [by_rows(g), by_rows(x), all_of(gain[None]), by_rows(dc)]
    ins += [by_rows(sw), all_of(sums), all_of(bgain[None]), all_of(bshift[None]), all_of(out_w)]
    outs = [out_rows((t, d), F32), out_all((1, d), F32), out_rows((t, part), F32)]
    outs += [out_all((2, part), F32), out_all((part, d), BF)]
    scratch = [pltpu.VMEM((part, d), F32)]
    return launch(conv_back_one_kernel, "conv_back_one", t // ROWS, place, ins, outs, scratch)


def conv_back_two_kernel(
    place, gbo, dc, gp, gp_lag, uc, link, valid, sums, ab, bgain, taps, *refs, groups
):
    blocks, (part, grad, taps_grad, gdc_s, glu_s, acc) = refs[:groups], refs[groups:]
    i = pl.program_id(0)
    width = dc.shape[1]
    clear_edges(gdc_s, glu_s)
    first_step(taps_grad, acc)

    @pl.when(i < pl.num_programs(0) - 1)
    def _():
        mu, rstd, count = batch_moments(sums)
        scaled = rstd * bgain[...]
        gvar = -0.5 * rstd * scaled * ab[1:2, :]
        mean_part = (-scaled * ab[0:1, :] - 2.0 * mu * gvar) / count
        slope_part = 2.0 * gvar / count
        gdc = gbo[...] * scaled + valid[...] * (mean_part + dc[...] * slope_part)
        keep_block(gdc_s, i, gdc)
        both = gp[...].astype(F32)
        keep_block(glu_s, i, both[:, :width] * jax.nn.sigmoid(both[:, width:]))

    @pl.when(i > 0)
    def _():
        gdc_rows, glu_rows = window(gdc_s, i - 1), window(glu_s, i - 1)
        middle = taken(gdc_rows, RIM)
        gglu = None
        for o in range(KER):
            linked = link[:, o : o + 1]
            mirror = KER - 1 - o
            term = taken(gdc_rows, o) * (linked * taps[mirror : mirror + 1, :])
            gglu = term if gglu is None else gglu + term
            taps_grad[o : o + 1, :] += jnp.sum(
                middle * (taken(glu_rows, o) * linked), axis=0, keepdims=True
            )
        both = gp_lag[...].astype(F32)
        opener = jax.nn.sigmoid(both[:, width:])
        first = gglu * opener
        second = first * both[:, :width] * (1.0 - opener)
        ggp = jnp.concatenate([first.astype(BF), second.astype(BF)], axis=1)
        n = blocks[0].shape[0]
        for s, w in enumerate(blocks):
            columns = columns_of(place, s, n)
            part[0, :, columns] = part[1, :, columns] = dot(ggp, w[...], 1, 1).astype(BF)
        acc[...] += dot(uc[...], ggp, 0, 0)

    @pl.when(last_step())
    def _():
        grad[...] = acc[...].astype(BF)


def conv_back_two(place, gbo, dc, gp, uc, link, valid, sums, ab, bgain, taps, blocks):
    t, d = uc.shape
    part = dc.shape[1]
    ins = [by_rows(gbo), by_rows(dc), by_rows(gp), by_rows(gp, 1), by_rows(uc, 1), by_rows(link, 1)]
    ins += [by_rows(valid), all_of(sums), all_of(ab), all_of(bgain[None]), all_of(taps)]
    ins += weight_blocks(blocks, 2 * part, 0)
    outs = [out_twice((t, d), BF, 1), out_all((d, 2 * part), BF), out_all((KER, part), F32)]
    scratch = [pltpu.VMEM((t + 2 * EDGE, part), F32)] * 2 + [pltpu.VMEM((d, 2 * part), F32)]
    kernel = functools.partial(conv_back_two_kernel, groups=len(blocks))
    return launch(kernel, "conv_back_two", t // ROWS + 1, place, ins, outs, scratch)


def context_back_kernel(place, p, r, g, x, gain, ctx, out_w, g_ref, gg, gctx, grad, acc):
    first_step(gg, acc)
    new = back_step(g, p, r, x, gain, gg)
    g_ref[...] = new
    low = new.astype(BF)
    gctx[...] = dot(low, out_w[...], 1, 1).astype(BF)
    acc[...] += dot(ctx[...], low, 0, 0)

    @pl.when(last_step())
    def _():
        grad[...] = acc[...].astype(BF)


def context_back(place, p, r, g, x, gain, ctx, out_w):
    t, d = x.shape
    part = ctx.shape[1]
    ins = two_parts(p, r) + [by_rows(g), by_rows(x), all_of(gain[None])]
    ins += [by_rows(ctx), all_of(out_w)]
    outs = [out_rows((t, d), F32), out_all((1, d), F32), out_rows((t, part), BF)]
    outs += [out_all((part, d), BF)]
    scratch = [pltpu.VMEM((part, d), F32)]
    return launch(context_back_kernel, "context_back", t // ROWS, place, ins, outs, scratch)


def projections_back_kernel(place, *refs, pieces, groups):
    parts, ua, refs = refs[:pieces], refs[pieces], refs[pieces + 1 :]
    blocks, (part, grad, acc) = refs[:groups], refs[groups:]
    first_step(acc)
    all3 = jnp.concatenate([p[...] for p in parts], axis=1)
    n = blocks[0].shape[0]
    for s, w in enumerate(blocks):
        columns = columns_of(place, s, n)
        part[0, :, columns] = part[1, :, columns] = dot(all3, w[...], 1, 1).astype(BF)
    acc[...] += dot(ua[...], all3, 0, 0)

    @pl.when(last_step())
    def _():
        grad[...] = acc[...].astype(BF)


def projections_back(place, *arrays):
    *parts, ua, blocks = arrays
    t, d = ua.shape
    part = sum(p.shape[1] for p in parts) // 3
    ins = [by_rows(p) for p in parts] + [by_rows(ua)] + weight_blocks(blocks, 3 * part, 1)
    outs = [out_twice((t, d), BF), out_all((d, 3 * part), BF)]
    scratch = [pltpu.VMEM((d, 3 * part), F32)]
    kernel = functools.partial(projections_back_kernel, pieces=len(parts), groups=len(blocks))
    return launch(kernel, "projections_back", t // ROWS, place, ins, outs, scratch)


def first_back_kernel(place, p, r, g, x, gain, out, gg):
    first_step(gg)
    out[...] = back_step(g, p, r, x, gain, gg).astype(BF)


def first_back(place, p, r, g, x, gain):
    t, d = x.shape
    ins = two_parts(p, r) + [by_rows(g), by_rows(x), all_of(gain[None])]
    outs = [out_rows((t, d), BF), out_all((1, d), F32)]
    return launch(first_back_kernel, "first_back", t // ROWS, place, ins, outs)


def encoding(length, features):
    half = features // 2
    frequency = jnp.exp(jnp.arange(half).astype(F32) * (-2.0 * math.log(10000.0) / features))
    fine = 32
    steps = jnp.arange(length // fine) * fine
    a = jnp.where(steps < length // 2, -steps, length - steps).astype(F32)[:, None] * frequency[None]
    b = jnp.arange(fine).astype(F32)[:, None] * frequency[None]
    sa, ca = jnp.sin(a)[:, None], jnp.cos(a)[:, None]
    sb, cb = jnp.sin(b)[None], jnp.cos(b)[None]
    sine = sa * cb - ca * sb
    cosine = ca * cb + sa * sb
    return jnp.concatenate([sine, cosine], axis=-1).reshape(length, features).astype(BF)


def on_device(
    frames,
    segment_ids,
    valid_mask,
    first_norm,
    first_up,
    first_down,
    attention_norm,
    query_proj,
    key_proj,
    value_proj,
    output_proj,
    position_proj,
    content_bias,
    position_bias,
    convolution_norm,
    pointwise_in,
    depthwise,
    batch_gain,
    batch_shift,
    pointwise_out,
    second_norm,
    second_up,
    second_down,
    final_norm,
    cotangent,
):
    groups = lax.axis_size("fsdp")
    member = lax.axis_index("fsdp")
    shard_frames, d = frames.shape[1:]
    t = segment_ids.shape[1]
    part = d // groups
    seg = segment_ids[0]
    valid = valid_mask[0].astype(F32)[:, None]
    bits = [bit_of(0), bit_of(1)]
    quarters = [1 - bits[0], 3 - bits[1], bits[0], 2 + bits[1]]
    owners = [lax.rem(member + groups - s, groups) for s in range(groups)]
    place = jnp.stack([(member + 1) % 2] + [jnp.int32(0)] * 3 + quarters + owners).astype(jnp.int32)

    def own(v, axis=0):
        return lax.dynamic_slice_in_dim(v, member * part, part, axis)

    def own_rows(v):
        return lax.dynamic_slice_in_dim(v, member * shard_frames, shard_frames, 0)[None]

    x0 = gather_rows(frames[0], place)
    seg_rim = jnp.pad(seg, (RIM, RIM), constant_values=-1)
    link = jnp.stack([(seg_rim[o : o + t] == seg).astype(F32) for o in range(KER)], axis=1)
    taps = own(depthwise).T
    gain_own, shift_own = own(batch_gain), own(batch_shift)

    if groups == 2:
        kept, away = packed(
            place,
            [(pointwise_in, 0, part), (pointwise_in, 2, part)]
            + [(m, 0, part) for m in (position_proj, query_proj, key_proj, value_proj)],
        )
        away, x0 = lax.optimization_barrier((away, x0))
        blocks = [kept, shifted(away, 1)]
    else:
        value_in, gate_in = pointwise_in[:, :d], pointwise_in[:, d:]
        blocks = own_columns(
            [(m, part) for m in (value_in, gate_in, position_proj, query_proj, key_proj, value_proj)]
        )
    part_sum, pre1, u1 = ffn_forward(place, x0, (), first_norm, first_up, first_down)
    other = pair_other(part_sum)
    encoded = encoding(t, d)
    pos = sum(
        dot(
            lax.dynamic_slice_in_dim(encoded, owner * part, part, 1),
            block[:, 2 * part : 3 * part],
        )
        for owner, block in zip(owners, blocks, strict=True)
    ).astype(BF)
    x1, ua, qc, qp, keys, values = qkv_forward(
        place, x0, part_sum, other, attention_norm, own(content_bias), own(position_bias), blocks
    )
    cotangent, _ = lax.optimization_barrier((cotangent, x1))
    cot = gather_rows(cotangent[0], place)
    ctx, part_sum = attention(place, seg, qc, qp, keys, values, pos, output_proj)
    other = pair_other(part_sum)
    x2, uc, gp, dc, sums = conv_forward(
        place, x1, part_sum, other, convolution_norm, link, valid, taps, blocks
    )
    sums = row_sum(sums)
    sw, part_sum = batch_forward(place, dc, sums, gain_own, shift_own, pointwise_out)
    other = pair_other(part_sum)
    x3, part_sum, pre2, u2 = ffn_forward(
        place, x2, (part_sum, other), second_norm, second_up, second_down
    )
    other = pair_other(part_sum)

    sequence = Sequence()
    run = sequence.run
    sums_of = {}
    plan = list(PLAN)

    def ready(name, arrays, parts=None):
        sums_of[name] = BatchSum(sequence, arrays, parts)
        if parts is not None:
            sums_of[name].step()

    def comm():
        for name in plan.pop(0):
            sums_of[name].step()

    hid = second_up.shape[0]
    layer_out, g, gf, final_gain, send0, send1 = final_down(
        place, x3, part_sum, other, cot, final_norm, pre2
    )
    keep = run(lambda *v: down_keep(place, *v), gf, pre2)
    ready("a", [hid], (tuple(keep), (send0, send1)))
    comm()
    part_sum, ga = run(lambda *v: ffn_back(place, *v), gf, pre2, second_up, second_down)
    comm()
    (part_sum,) = sequence.tie(part_sum)
    other = pair_swap(part_sum)
    quads = run(lambda *v: up_grad(place, *v), ga, u2)
    comm()
    g, second_gain, gbo, ab, out_w_grad = run(
        lambda *v: conv_back_one(place, *v),
        part_sum, other, g, x3, second_norm, dc, sw, sums, gain_own, shift_own, pointwise_out,
    )
    comm()
    (ab,) = sequence.tie(ab)
    ab = row_sum(ab)
    sequence.last = ab
    comm()
    quads = sequence.tie(*quads)
    ready("b", [hid], ((quads[2], quads[3]), (quads[0], quads[1])))
    part_sum, in_w_grad, taps_grad = run(
        lambda ab, gbo: conv_back_two(
            place, gbo, dc, gp, uc, link, valid, sums, ab, gain_own, taps, blocks
        ),
        ab,
        gbo,
    )
    comm()
    part_sum, in_w_grad = sequence.tie(part_sum, in_w_grad)
    other = pair_swap(part_sum)
    swapped = row_blocks_swap(in_w_grad)

    def unfold(swapped, at):
        columns = slice(at * part, (at + 1) * part)
        return jnp.concatenate([swapped[j][:, columns] for j in range(groups)], axis=1)

    ready("c", [out_w_grad, unfold(swapped, 0), unfold(swapped, 1)])
    comm()
    g, conv_gain, gctx, output_grad = run(
        lambda *v: context_back(place, *v),
        part_sum, other, g, x2, convolution_norm, ctx, output_proj,
    )
    comm()
    halves_of = []
    for first in (True, False):
        half = run(
            lambda *v, first=first: attention_back(place, seg, *v, first),
            qc, qp, keys, values, pos, gctx,
        )
        if half is not None:
            halves_of.append(half)
        comm()
    gqkv = [h[at] for at in range(3) for h in halves_of]
    gpos, content_grad, position_grad = (
        jnp.concatenate([h[at] for h in halves_of], axis=1) for at in range(3, 6)
    )
    part_sum, qkv_grad = run(lambda *v: projections_back(place, *v, blocks), *gqkv, ua)
    comm()
    part_sum, qkv_grad = sequence.tie(part_sum, qkv_grad)
    other = pair_swap(part_sum)
    high = gpos.astype(BF)
    low = (gpos - high.astype(F32)).astype(BF)
    pos_grad = (dot(encoded, high, 0, 0) + dot(encoded, low, 0, 0)).astype(BF)
    swapped = row_blocks_swap(jnp.concatenate([qkv_grad, pos_grad], axis=1))
    ready("d", [output_grad] + [unfold(swapped, at) for at in range(4)])
    comm()
    g, gf, attention_gain, *quads = run(
        lambda *v: back_down(place, *v), part_sum, other, g, x1, attention_norm, pre1
    )
    ready("e", [hid], ((quads[2], quads[3]), (quads[0], quads[1])))
    comm()
    part_sum, ga = run(lambda *v: ffn_back(place, *v), gf, pre1, first_up, first_down)
    comm()
    (part_sum,) = sequence.tie(part_sum)
    other = pair_swap(part_sum)
    quads = run(lambda *v: up_grad(place, *v), ga, u1)
    ready("f", [hid], ((quads[2], quads[3]), (quads[0], quads[1])))
    comm()
    frames_grad, first_gain = run(
        lambda *v: first_back(place, *v), part_sum, other, g, x0, first_norm
    )
    gains = [own(v[0]) for v in (first_gain, attention_gain, conv_gain, second_gain, final_gain)]
    small = jnp.concatenate(
        [jnp.stack(gains), content_grad, position_grad, taps_grad], axis=0
    )
    sums_of["s"] = SmallSum(sequence, small)
    comm()
    for job in sums_of.values():
        job.finish()
    small = sums_of["s"].v
    out_w_grad, value_grad, gate_grad = sums_of["c"].out
    output_grad, q_grad, k_grad, v_grad, pos_grad = sums_of["d"].out
    return (
        own_rows(layer_out),
        own_rows(frames_grad),
        small[0],
        sums_of["f"].out[0],
        sums_of["e"].out[0],
        small[1],
        q_grad,
        k_grad,
        v_grad,
        output_grad,
        pos_grad,
        small[5],
        small[6],
        small[2],
        jnp.concatenate([value_grad, gate_grad], axis=1),
        small[7:].T,
        ab[1],
        ab[0],
        out_w_grad,
        small[3],
        sums_of["b"].out[0],
        sums_of["a"].out[0],
        small[4],
    )


def solution(mesh):
    rows, shard, whole = P("batch", "fsdp", None), P("fsdp", None), P()
    return jax.shard_map(
        on_device,
        mesh=mesh,
        in_specs=(
            rows,
            P("batch", None),
            P("batch", None),
            whole,
            shard,
            shard,
            whole,
            shard,
            shard,
            shard,
            shard,
            shard,
            whole,
            whole,
            whole,
            shard,
            whole,
            whole,
            whole,
            shard,
            whole,
            shard,
            shard,
            whole,
            rows,
        ),
        out_specs=(
            rows,
            rows,
            P("fsdp"),
            shard,
            shard,
            P("fsdp"),
            shard,
            shard,
            shard,
            shard,
            shard,
            P("fsdp"),
            P("fsdp"),
            P("fsdp"),
            shard,
            shard,
            P("fsdp"),
            P("fsdp"),
            shard,
            P("fsdp"),
            shard,
            shard,
            P("fsdp"),
        ),
        check_vma=False,
    )
```
